256 devices in a mesh: dp: 16 (over z, core), graph: 16 (over y, x).
Axes of the slice: x: 4, y: 4, z: 8, core: 2. Of those that a mesh axis runs over, the one named last changes fastest.
Arguments:
- node_feats: bfloat16 [16, 256, 3200], P('dp', 'graph'), may hold values from -6 to 6
- source: int32 [16, 2048], P('dp', 'graph'), may hold values from 0 to 255
- target: int32 [16, 2048], P('dp', 'graph'), may hold values from 0 to 255
- rotation: bfloat16 [16, 165, 2048], P('dp', None, 'graph'), may hold values from -6 to 6
- radial: bfloat16 [16, 2048, 640], P('dp', 'graph'), may hold values from 0.25 to 1.75
- edge_count: int32 [16, 16], P('dp', 'graph'), may hold values from 16 to 128, as said below
- cotangent: bfloat16 [16, 256, 3200], P('dp', 'graph'), may hold values from -6 to 6
- weight_zero: bfloat16 [640, 640], replicated, may hold values from -0.25 to 0.25
- weight_first: bfloat16 [2, 512, 512], replicated, may hold values from -0.1875 to 0.1875
- weight_second: bfloat16 [2, 384, 384], replicated, may hold values from -0.21875 to 0.21875
Outputs:
- node_out: bfloat16 [16, 256, 3200], P('dp', 'graph')
- node_grad: bfloat16 [16, 256, 3200], P('dp', 'graph')
- grad_zero: float32 [640, 640], replicated
- grad_first: float32 [2, 512, 512], replicated
- grad_second: float32 [2, 384, 384], replicated
The draws below stay inside these ranges and needn't reach their ends.
Inputs may be any that keep to these rules, and one draw needn't show every extreme that they name: In each device's 128 slots the first edge_count are live; in every batch some index of graph has all 128 live.
All inputs are finite; a program needn't handle non-finite values.
Results may differ from the reference program's by a relative error of at most 0.019.
Values may be sent and summed in bfloat16 or wider, within the bound.
A program may use at most 128 MiB of HBM per device.

```python
import math
import jax
import jax.numpy as jnp
import numpy as np
from jax import lax

C = 128
EDGE_DEV = 128
NODES = 256
EDGES = 2048
BATCHES = 16
N_GRAPH = 16


def draw_edge_count(key, part):
    key = jax.random.fold_in(key, 5)
    first_key, second_key = jax.random.split(key)
    counts = jax.random.randint(first_key, (BATCHES, N_GRAPH), EDGE_DEV // 8, EDGE_DEV + 1)
    busiest = jax.random.randint(second_key, (BATCHES, 1), 0, N_GRAPH)
    column = jnp.arange(N_GRAPH, dtype=jnp.int32)[None, :]
    return jnp.where(column == busiest, EDGE_DEV, counts).astype(jnp.int32)


def place_ends(result, key, smallest, top_value):
    spot = [jax.random.randint(jax.random.fold_in(key, axis), (), 0, length) for axis, length in enumerate(result.shape)]
    main_axis = result.shape.index(max(result.shape))
    next_to = spot[:main_axis] + [(spot[main_axis] + 1) % result.shape[main_axis]] + spot[main_axis + 1:]
    return result.at[tuple(spot)].set(smallest).at[tuple(next_to)].set(top_value)


def block_levels(stream_key, extent, cuts, low, top_value):
    def one(dim, blocks):
        steps = jax.random.uniform(jax.random.fold_in(jax.random.fold_in(stream_key, 6), dim), (blocks,), jnp.float32, low / len(cuts), top_value / len(cuts))
        return jnp.repeat(jnp.exp(steps), extent[dim] // blocks).reshape((-1,) + (1,) * (len(extent) - dim - 1))

    loudness = one(*cuts[0])
    for cut in cuts[1:]:
        loudness = loudness * one(*cut)
    return loudness


def gaussian(own_key, extent, spread, reach, pieces=(), kind=jnp.bfloat16):
    entries = spread * jax.random.normal(own_key, extent, jnp.float32)
    if pieces:
        entries = entries * block_levels(own_key, extent, pieces, -0.22, 0.18)
    return jnp.clip(entries, -reach, reach).astype(kind)


def setup_inputs(seed: int = 0) -> dict:
    key_list = jax.random.split(jax.random.key(seed), 11)
    node_feats = gaussian(key_list[0], (BATCHES, NODES, 25 * C), 1.0, 6.0, ((0, 16), (1, 16)))
    source = place_ends(jax.random.randint(key_list[1], (BATCHES, EDGES), 0, NODES), jax.random.fold_in(key_list[1], 1), 0, NODES - 1).astype(jnp.int32)
    target = place_ends(jax.random.randint(key_list[2], (BATCHES, EDGES), 0, NODES), jax.random.fold_in(key_list[2], 1), 0, NODES - 1).astype(jnp.int32)
    rotation = gaussian(key_list[3], (BATCHES, 165, EDGES), 1.0, 6.0, ((0, 16), (2, 16)))
    radial = jnp.clip(0.25 + 1.5 * jax.random.uniform(key_list[4], (BATCHES, EDGES, 5 * C), jnp.float32) ** block_levels(key_list[4], (BATCHES, EDGES, 5 * C), ((0, 16), (1, 16)), -0.2, 0.2), 0.25, 1.75).astype(jnp.bfloat16)
    edge_count = draw_edge_count(jax.random.fold_in(key_list[10], 71), 0)
    cotangent = gaussian(key_list[6], (BATCHES, NODES, 25 * C), 1.0, 6.0, ((0, 16), (1, 16)))
    weight_zero = gaussian(key_list[7], (5 * C, 5 * C), (5 * C) ** -0.5, 0.25)
    weight_first = gaussian(key_list[8], (2, 4 * C, 4 * C), (8 * C) ** -0.5, 0.1875)
    weight_second = gaussian(key_list[9], (2, 3 * C, 3 * C), (6 * C) ** -0.5, 0.21875)
    return dict(node_feats=node_feats, source=source, target=target, rotation=rotation, radial=radial, edge_count=edge_count, cotangent=cotangent, weight_zero=weight_zero, weight_first=weight_first, weight_second=weight_second)


ZERO_ORDER = [0, 2, 6, 12, 20]
PLUS_FIRST = [3, 7, 13, 21]
MINUS_FIRST = [1, 5, 11, 19]
PLUS_SECOND = [8, 14, 22]
MINUS_SECOND = [4, 10, 18]
DEGREE_INDEX = [0] + [1] * 3 + [2] * 5 + [3] * 7 + [4] * 9

def rotate_blocks(values, rotation, transposed):
    results = []
    offset = 0
    for degree in range(5):
        order_size = 2 * degree + 1
        rot_block = rotation[offset:offset + order_size * order_size].reshape(order_size, order_size, -1).astype(jnp.float32)
        coef_piece = values[:, degree * degree:(degree + 1) * (degree + 1), :].astype(jnp.float32)
        pattern = 'jie,ejc->eic' if transposed else 'ije,ejc->eic'
        results.append(jnp.einsum(pattern, rot_block, coef_piece) / math.sqrt(order_size))
        offset += order_size * order_size
    return jnp.concatenate(results, axis=1)

def pick_rows(values, indices):
    return values[:, np.array(indices), :].reshape(values.shape[0], len(indices) * values.shape[2])

def join_groups(groups, channels):
    edge_rows = groups[0][1].shape[0]
    columns = [jnp.zeros((edge_rows, channels), jnp.float32)] * 25
    for indices, array in groups:
        shaped = array.reshape(edge_rows, len(indices), channels)
        for position, coef_index in enumerate(indices):
            columns[coef_index] = shaped[:, position, :]
    return jnp.stack(columns, axis=1)

def contract_rows(left, right):
    return lax.dot_general(left, right, (((0,), (0,)), ((), ())), preferred_element_type=jnp.float32)

def times_transposed(left, weight):
    return lax.dot_general(left, weight, (((1,), (1,)), ((), ())), preferred_element_type=jnp.float32)

def plane_forward(active, weight_zero, weight_first, weight_second):
    channels = active.shape[2]
    zero_part = pick_rows(active, ZERO_ORDER)
    plus_one = pick_rows(active, PLUS_FIRST)
    minus_one = pick_rows(active, MINUS_FIRST)
    plus_two = pick_rows(active, PLUS_SECOND)
    minus_two = pick_rows(active, MINUS_SECOND)
    out_zero = jnp.dot(zero_part, weight_zero, preferred_element_type=jnp.float32)
    out_plus_one = jnp.dot(plus_one, weight_first[0], preferred_element_type=jnp.float32) - jnp.dot(minus_one, weight_first[1], preferred_element_type=jnp.float32)
    out_minus_one = jnp.dot(minus_one, weight_first[0], preferred_element_type=jnp.float32) + jnp.dot(plus_one, weight_first[1], preferred_element_type=jnp.float32)
    out_plus_two = jnp.dot(plus_two, weight_second[0], preferred_element_type=jnp.float32) - jnp.dot(minus_two, weight_second[1], preferred_element_type=jnp.float32)
    out_minus_two = jnp.dot(minus_two, weight_second[0], preferred_element_type=jnp.float32) + jnp.dot(plus_two, weight_second[1], preferred_element_type=jnp.float32)
    return join_groups([(ZERO_ORDER, out_zero), (PLUS_FIRST, out_plus_one), (MINUS_FIRST, out_minus_one), (PLUS_SECOND, out_plus_two), (MINUS_SECOND, out_minus_two)], channels)

def plane_backward(active, upstream, weight_zero, weight_first, weight_second):
    channels = active.shape[2]
    zero_part = pick_rows(active, ZERO_ORDER)
    plus_one = pick_rows(active, PLUS_FIRST)
    minus_one = pick_rows(active, MINUS_FIRST)
    plus_two = pick_rows(active, PLUS_SECOND)
    minus_two = pick_rows(active, MINUS_SECOND)
    up_zero = pick_rows(upstream, ZERO_ORDER)
    up_plus_one = pick_rows(upstream, PLUS_FIRST)
    up_minus_one = pick_rows(upstream, MINUS_FIRST)
    up_plus_two = pick_rows(upstream, PLUS_SECOND)
    up_minus_two = pick_rows(upstream, MINUS_SECOND)
    grad_zero = contract_rows(zero_part, up_zero)
    grad_first = jnp.stack([contract_rows(plus_one, up_plus_one) + contract_rows(minus_one, up_minus_one), contract_rows(plus_one, up_minus_one) - contract_rows(minus_one, up_plus_one)])
    grad_second = jnp.stack([contract_rows(plus_two, up_plus_two) + contract_rows(minus_two, up_minus_two), contract_rows(plus_two, up_minus_two) - contract_rows(minus_two, up_plus_two)])
    back_zero = times_transposed(up_zero, weight_zero)
    back_plus_one = times_transposed(up_plus_one, weight_first[0]) + times_transposed(up_minus_one, weight_first[1])
    back_minus_one = times_transposed(up_minus_one, weight_first[0]) - times_transposed(up_plus_one, weight_first[1])
    back_plus_two = times_transposed(up_plus_two, weight_second[0]) + times_transposed(up_minus_two, weight_second[1])
    back_minus_two = times_transposed(up_minus_two, weight_second[0]) - times_transposed(up_plus_two, weight_second[1])
    d_active = join_groups([(ZERO_ORDER, back_zero), (PLUS_FIRST, back_plus_one), (MINUS_FIRST, back_minus_one), (PLUS_SECOND, back_plus_two), (MINUS_SECOND, back_minus_two)], channels)
    return (d_active, (grad_zero, grad_first, grad_second))

def device_sum(values, indices, nodes):
    shaped = values.reshape(N_GRAPH, -1, values.shape[1])
    shaped_ids = indices.reshape(N_GRAPH, -1)

    def add_device(total, pair):
        partial_sum = jax.ops.segment_sum(pair[0].astype(jnp.float32), pair[1], num_segments=nodes)
        rounded = lax.optimization_barrier(partial_sum.astype(jnp.bfloat16))
        return (total + rounded.astype(jnp.float32), None)
    total, unused = lax.scan(add_device, jnp.zeros((nodes, values.shape[1]), jnp.float32), (shaped, shaped_ids))
    return total.astype(jnp.bfloat16)

def reference(node_feats, source, target, rotation, radial, edge_count, cotangent, weight_zero, weight_first, weight_second):

    def one_batch(inputs):
        feats, sources, targets, rotations, radials, counts, cotangents = inputs
        edges = sources.shape[0]
        edge_dev = edges // N_GRAPH
        nodes = feats.shape[0]
        channels = feats.shape[1] // 25
        slots = jnp.arange(edges, dtype=jnp.int32)
        live = (slots % edge_dev < counts[slots // edge_dev]).astype(jnp.float32)
        gathered = feats[sources].reshape(edges, 25, channels)
        radial_full = radials.reshape(edges, 5, channels)[:, np.array(DEGREE_INDEX), :].astype(jnp.float32)
        active = (rotate_blocks(gathered, rotations, False) * radial_full).astype(jnp.bfloat16)
        edge_msg = plane_forward(active, weight_zero, weight_first, weight_second).astype(jnp.bfloat16)
        message = (rotate_blocks(edge_msg, rotations, True) * live[:, None, None]).astype(jnp.bfloat16)
        out_rows = device_sum(message.reshape(edges, 25 * channels), targets, nodes)
        picked = (cotangents[targets].astype(jnp.float32) * live[:, None]).astype(jnp.bfloat16).reshape(edges, 25, channels)
        upstream = rotate_blocks(picked, rotations, False).astype(jnp.bfloat16)
        d_active, grads = plane_backward(active, upstream, weight_zero, weight_first, weight_second)
        back = (d_active * radial_full).astype(jnp.bfloat16)
        edge_grad = rotate_blocks(back, rotations, True).astype(jnp.bfloat16).reshape(edges, 25 * channels)
        grad_rows = device_sum(edge_grad, sources, nodes)
        return (out_rows, grad_rows, grads)
    node_out, node_grad, grads = lax.map(one_batch, (node_feats, source, target, rotation, radial, edge_count, cotangent))
    scale = 1.0 / math.sqrt(BATCHES * EDGES)
    return (node_out, node_grad, lax.optimization_barrier(jnp.sum(grads[0], axis=0)) * scale, lax.optimization_barrier(jnp.sum(grads[1], axis=0)) * scale, lax.optimization_barrier(jnp.sum(grads[2], axis=0)) * scale)
```

```python
import functools, math
import jax, jax.numpy as jnp, numpy as np
from jax import lax
from jax.experimental import pallas as pl
from jax.experimental.pallas import tpu as pltpu
from jax.sharding import PartitionSpec as P

C = 128
E = 128
N = 256
W = 25 * C
F32, BF16 = jnp.float32, jnp.bfloat16
OFF = [0, 1, 10, 35, 84]


def dot(a, b):
    return lax.dot_general(a, b, (((1,), (0,)), ((), ())), preferred_element_type=F32)


def dot_nt(a, b):
    return lax.dot_general(a, b, (((1,), (1,)), ((), ())), preferred_element_type=F32)


def dot_tn(a, b):
    return lax.dot_general(a, b, (((0,), (0,)), ((), ())), preferred_element_type=F32)


def orders(l):
    top = min(l, 2)
    return range(-top, top + 1)


def kept(l):
    return sum(len(orders(q)) * (2 * q + 1) for q in range(l))


def prepare(src, dst, count, rot, oh_s, oh_d, oh_st, oh_dt, rot_t):
    node = lax.broadcasted_iota(jnp.int32, (N, E), 0)
    slot = lax.broadcasted_iota(jnp.int32, (N, E), 1)
    s = (node == src).astype(F32)
    d = ((node == dst) & (slot < count)).astype(F32)
    oh_st[...] = s.astype(BF16)
    oh_dt[...] = d.astype(BF16)
    oh_s[...] = s.T.astype(BF16)
    oh_d[...] = d.T.astype(BF16)
    eye = (lax.broadcasted_iota(jnp.int32, (E, E), 0) == lax.broadcasted_iota(jnp.int32, (E, E), 1)).astype(BF16)
    k = lax.broadcasted_iota(jnp.int32, (1, 165), 1)
    scale = jnp.ones((1, 165), F32)
    for l in range(1, 5):
        scale = jnp.where(k >= OFF[l], 1.0 / math.sqrt(2 * l + 1), scale)
    rot_t[:, :165] = dot_nt(eye, rot) * scale


def group_slot(l, m):
    return abs(m), (E if m < 0 else 0), (l - abs(m)) * C


def rotate_in(l, feats, cots, oh_s, oh_d, rad, rot_t, x_buf, u_buf, wide, act, ups, ups_s):
    size = 2 * l + 1
    x_buf[:, : size * C] = dot(oh_s[...], feats)
    u_buf[:, : size * C] = dot(oh_d[...], cots)

    @pl.loop(0, E // 16)
    def _(b):
        r = pl.multiple_of(b * 16, 16)
        rows = pl.ds(r, 16)
        rt = rot_t[rows, :]
        xs = [x_buf[rows, j * C : (j + 1) * C] for j in range(size)]
        us = [u_buf[rows, j * C : (j + 1) * C] for j in range(size)]
        rd = rad[rows, l * C : (l + 1) * C].astype(F32)
        at = kept(l)
        for m in orders(l):
            a = u = None
            for j in range(size):
                k = OFF[l] + (m + l) * size + j
                w = jnp.broadcast_to(rt[:, k : k + 1], (16, C))
                wide[at, rows, :] = w
                at += 1
                a = w * xs[j] if a is None else a + w * xs[j]
                u = w * us[j] if u is None else u + w * us[j]
            g, ro, co = group_slot(l, m)
            here = pl.ds(r + ro, 16)
            cols = slice(co, co + C)
            act[g][here, cols] = (a * rd).astype(BF16)
            ub = u.astype(BF16)
            ups[g][here, cols] = ub
            if g:
                there = pl.ds(r + E - ro, 16)
                ups_s[g][there, cols] = ub if m < 0 else -ub


def plane(act, ups, ws, msg, back):
    msg[0][...] = dot(act[0][...], ws[0][...])
    back[0][...] = dot_nt(ups[0][...], ws[0][...])
    for g in (1, 2):
        a = act[g][...]
        y0 = dot(a, ws[g][0])
        y1 = dot(a, ws[g][1])
        msg[g][:E, :] = y0[:E] - y1[E:]
        msg[g][E:, :] = y0[E:] + y1[:E]
        u = ups[g][...]
        z0 = dot_nt(u, ws[g][0])
        z1 = dot_nt(u, ws[g][1])
        back[g][:E, :] = z0[:E] + z1[E:]
        back[g][E:, :] = z0[E:] - z1[:E]


def rotate_out(l, msg, back, rad, wide, oh_st, oh_dt, m_buf, e_buf, out, grad):
    size = 2 * l + 1

    @pl.loop(0, E // 16)
    def _(b):
        r = pl.multiple_of(b * 16, 16)
        rows = pl.ds(r, 16)
        rd = rad[rows, l * C : (l + 1) * C].astype(F32)
        ms, bs = [], []
        for m in orders(l):
            g, ro, co = group_slot(l, m)
            here = pl.ds(r + ro, 16)
            ms.append(msg[g][here, co : co + C])
            bs.append(back[g][here, co : co + C] * rd)
        n = len(ms)
        for i in range(size):
            a = u = None
            for j in range(n):
                w = wide[kept(l) + j * size + i, rows, :]
                a = w * ms[j] if a is None else a + w * ms[j]
                u = w * bs[j] if u is None else u + w * bs[j]
            m_buf[rows, i * C : (i + 1) * C] = a.astype(BF16)
            e_buf[rows, i * C : (i + 1) * C] = u.astype(BF16)

    cols = slice(l * l * C, (l + 1) * (l + 1) * C)
    out[:, cols] = dot(oh_dt[...], m_buf[:, : size * C]).astype(BF16)
    grad[:, cols] = dot(oh_st[...], e_buf[:, : size * C]).astype(BF16)


def weight_grads(act, ups, ups_s, flat):
    scale = 1.0 / math.sqrt(32768)
    at = 0
    for g in range(3):
        left = act[g][...].T
        for right in (ups, ups_s)[: 1 if g == 0 else 2]:
            total = (dot(left, right[g][...]) * scale).astype(BF16)
            rows = total.shape[0]
            for c in range(rows // C):
                flat[at : at + rows // 16] = total[:, c * C : (c + 1) * C].reshape(rows // 16, 16, C)
                at += rows // 16
    flat[600:608] = jnp.zeros((8, 16, C), BF16)


def compute_kernel(count, src, dst, rot, rad, feats, cots, w0, w1, w2, out, grad, flat,
                   oh_s, oh_d, oh_st, oh_dt, rot_t, x_buf, u_buf, wide, a0, a1, a2, u0, u1, u2, v1, v2,
                   m0, m1, m2, b0, b1, b2, mb, eb):
    prepare(src[...], dst[...], count[0, 0], rot[...], oh_s, oh_d, oh_st, oh_dt, rot_t)
    act, ups, ups_s = (a0, a1, a2), (u0, u1, u2), (None, v1, v2)
    ws, msg, back = (w0, w1, w2), (m0, m1, m2), (b0, b1, b2)
    for l in range(5):
        cols = slice(l * l * C, (l + 1) * (l + 1) * C)
        rotate_in(l, feats[:, cols], cots[:, cols], oh_s, oh_d, rad, rot_t, x_buf, u_buf, wide, act, ups, ups_s)
    weight_grads(act, ups, ups_s, flat)
    plane(act, ups, ws, msg, back)
    for l in range(5):
        rotate_out(l, msg, back, rad, wide, oh_st, oh_dt, mb, eb, out, grad)


def compute(count, src, dst, rot, rad, feats, cots, w0, w1, w2):
    v = pl.BlockSpec(memory_space=pltpu.VMEM)
    V = pltpu.VMEM
    return pl.pallas_call(
        compute_kernel,
        out_shape=(
            jax.ShapeDtypeStruct((N, W), BF16), jax.ShapeDtypeStruct((N, W), BF16),
            jax.ShapeDtypeStruct((608, 16, C), BF16)),
        in_specs=[pl.BlockSpec(memory_space=pltpu.SMEM)] + [v] * 9,
        out_specs=(v,) * 3,
        scratch_shapes=[
            V((E, N), BF16), V((E, N), BF16), V((N, E), BF16), V((N, E), BF16), V((E, 256), F32),
            V((E, 9 * C), F32), V((E, 9 * C), F32), V((115, E, C), F32),
            V((E, 640), BF16), V((2 * E, 512), BF16), V((2 * E, 384), BF16),
            V((E, 640), BF16), V((2 * E, 512), BF16), V((2 * E, 384), BF16),
            V((2 * E, 512), BF16), V((2 * E, 384), BF16),
            V((E, 640), F32), V((2 * E, 512), F32), V((2 * E, 384), F32),
            V((E, 640), F32), V((2 * E, 512), F32), V((2 * E, 384), F32),
            V((E, 9 * C), BF16), V((E, 9 * C), BF16),
        ],
        compiler_params=pltpu.CompilerParams(vmem_limit_bytes=56 * 2**20),
        name="edge_block",
    )(count, src, dst, rot, rad, feats, cots, w0, w1, w2)

MESH = pl.DeviceIdType.MESH
TILES = 304
PIECE = 38


def start_at(g):
    return lax.div(g * 35, 15) if not isinstance(g, int) else g * 35 // 15


def wrap(p, d, n):
    return lax.rem(p + (d % n), n)


class Place:
    def __init__(self):
        g, p = lax.axis_index("graph"), lax.axis_index("dp")
        self.g, self.p = g, p
        self.y, self.x = lax.div(g, 4), lax.rem(g, 4)
        self.z, self.c = lax.div(p, 2), lax.rem(p, 2)

    def plane(self, dy, dx):
        return (self.p, wrap(self.y, dy, 4) * 4 + wrap(self.x, dx, 4))

    def peer(self, d):
        return (self.p, wrap(self.g, d, 16))

    def up(self, d):
        return (wrap(self.z, d, 8) * 2 + self.c, self.g)

    def sibling(self):
        return (self.z * 2 + 1 - self.c, self.g)


def greet(devices):
    barrier = pltpu.get_barrier_semaphore()
    for d in devices:
        pl.semaphore_signal(barrier, inc=1, device_id=d, device_id_type=MESH)
    pl.semaphore_wait(barrier, len(devices))


class Sender:
    def __init__(self, send, recv):
        self.send, self.recv, self.next, self.all = send, recv, 0, []

    def make(self, src, dst, to):
        k = self.next
        self.next += 1
        c = pltpu.make_async_remote_copy(src_ref=src, dst_ref=dst, send_sem=self.send.at[k], recv_sem=self.recv.at[k],
                                         device_id=to, device_id_type=MESH)
        self.all.append(c)
        return c

    def go(self, src, dst, to):
        c = self.make(src, dst, to)
        c.start()
        return c

    def finish(self):
        for c in self.all:
            c.wait_send()


def interleave(streams):
    streams = list(streams)
    while streams:
        left = []
        for s in streams:
            try:
                next(s)
                left.append(s)
            except StopIteration:
                pass
        streams = left


def gather_stream(snd, at, dev, done=lambda da, db: None):
    def spread(da):
        return [snd.go(at(da, 0, None), at(da, 0, None), dev(0, s)) for s in (1, -1)]

    def relay(da, got):
        for k, s in enumerate((1, -1)):
            yield
            got[k].wait_recv()
            done(da, -s)
            last.append(snd.go(at(da, -s, k), at(da, -s, k), dev(0, s)))

    last = []
    first = [snd.go(at(0, 0, None), at(0, 0, None), dev(s, 0)) for s in (1, -1)]
    second = {0: spread(0)}
    done(0, 0)
    far = []
    for k, s in enumerate((1, -1)):
        yield
        first[k].wait_recv()
        far.append(snd.go(at(-s, 0, k), at(-s, 0, k), dev(s, 0)))
        second[-s] = spread(-s)
        done(-s, 0)
    yield from relay(0, second[0])
    yield
    for f in far:
        f.wait_recv()
    second[2] = spread(2)
    done(2, 0)
    for da in (-1, 1, 2):
        yield from relay(da, second[da])
    for i, da in enumerate((0, -1, 1, 2)):
        yield
        last[2 * i].wait_recv()
        last[2 * i + 1].wait_recv()
        done(da, 2)


CHUNKS = ((0, 9), (9, 16), (16, 25))


def col_at(buf, pl_, lo, hi, y_first):
    mid = (lo + hi) // 2
    parts = {None: (lo, hi), 0: (lo, mid), 1: (mid, hi)}

    def at(da, db, part):
        dy, dx = (da, db) if y_first else (db, da)
        a, b = parts[part]
        return buf.at[wrap(pl_.y, dy, 4), wrap(pl_.x, dx, 4), :, a * C : b * C]
    return at


def plane_dev(pl_, y_first):
    return (lambda da, db: pl_.plane(da, db)) if y_first else (lambda da, db: pl_.plane(db, da))


def gather_kernel(chunks, f_in, c_in, f_out, c_out, send, recv):
    here = Place()
    greet([here.plane(*d) for d in ((0, 1), (0, -1), (1, 0), (-1, 0))])
    f_out[here.y, here.x] = f_in[0]
    c_out[here.y, here.x] = c_in[0]
    snd = Sender(send, recv)
    streams = []
    for lo, hi in chunks:
        for buf, yf in ((f_out, False), (c_out, True)):
            streams.append(gather_stream(snd, col_at(buf, here, lo, hi, yf), plane_dev(here, yf)))
    interleave(streams)
    snd.finish()


def gather(feats, cots, chunks=CHUNKS):
    v = pl.BlockSpec(memory_space=pltpu.VMEM)
    n = 20 * 2 * len(chunks)
    o = jax.ShapeDtypeStruct((4, 4, 16, W), BF16)
    f, c = pl.pallas_call(
        functools.partial(gather_kernel, chunks),
        out_shape=(o, o), in_specs=[v, v], out_specs=(v, v),
        scratch_shapes=[pltpu.SemaphoreType.DMA((n,)), pltpu.SemaphoreType.DMA((n,))],
        compiler_params=pltpu.CompilerParams(collective_id=0, has_side_effects=True, vmem_limit_bytes=32 * 2**20),
        name="gather_nodes",
    )(feats, cots)
    return f.reshape(N, W), c.reshape(N, W)


def add(*xs):
    t = xs[0].astype(F32)
    for x in xs[1:]:
        t = t + x.astype(F32)
    return t.astype(BF16)


def scatter_stream(snd, part, mid, t, r, q, t2, r2, out, here, lo, hi, y_first):
    cm = (lo + hi) // 2
    full, halves = slice(lo * C, hi * C), (slice(lo * C, cm * C), slice(cm * C, hi * C))
    a, b = (here.y, here.x) if y_first else (here.x, here.y)
    dev = plane_dev(here, y_first)

    def row(da, cols):
        i = wrap(a, da, 4)
        return part.at[i, :, :, cols] if y_first else part.at[:, i, :, cols]

    got = [snd.go(row(2, halves[k]), t.at[k, :, :, halves[k]], dev(s, 0)) for k, s in enumerate((1, -1))]
    sent = []
    for k, s in enumerate((1, -1)):
        yield
        got[k].wait_recv()
        mid[k, :, :, halves[k]] = add(row(s, halves[k])[...], t[k, :, :, halves[k]])
        mid[k, :, :, halves[1 - k]] = row(s, halves[1 - k])[...]
        sent.append(snd.go(mid.at[k, :, :, full], r.at[k, :, :, full], dev(s, 0)))
    yield
    sent[0].wait_recv()
    sent[1].wait_recv()
    q[:, :, full] = add(row(0, full)[...], r[0, :, :, full], r[1, :, :, full])
    far = wrap(b, 2, 4)
    got = [snd.go(q.at[far, :, halves[k]], t2.at[k, :, halves[k]], dev(0, s)) for k, s in enumerate((1, -1))]
    sent = []
    for k, s in enumerate((1, -1)):
        yield
        got[k].wait_recv()
        i = wrap(b, s, 4)
        q[i, :, halves[k]] = add(q[i, :, halves[k]], t2[k, :, halves[k]])
        sent.append(snd.go(q.at[i, :, full], r2.at[k, :, full], dev(0, s)))
    yield
    sent[0].wait_recv()
    sent[1].wait_recv()
    out[0, :, full] = add(q[b, :, full], r2[0, :, full], r2[1, :, full])


def swap_cores(snd, flat, sib, here):
    other = (1 - here.c) * TILES
    copies = {}
    for d in (-1, 1, -2, 2, -3, 3, 4, 0):
        k = wrap(here.z, d, 8) * PIECE
        copies[d % 8] = snd.go(flat.at[pl.ds(other + k, PIECE)], sib.at[pl.ds(k, PIECE)], here.sibling())
    return copies


def z_stream(snd, copies, seen, flat, sib, box, outbox, zsum, here, sign, lo, hi):
    def mine(d):
        if d not in seen:
            seen.add(d)
            copies[d].wait_recv()
        k = wrap(here.z, d, 8) * PIECE + lo
        return flat[pl.ds(here.c * TILES + k, hi - lo)], sib[pl.ds(k, hi - lo)]

    got = None
    for s in range(7):
        yield
        terms = mine((-sign * (1 + s)) % 8)
        if got is not None:
            got.wait_recv()
            terms += (box[s - 1, lo:hi],)
        outbox[s, lo:hi] = add(*terms)
        got = snd.go(outbox.at[s, lo:hi], box.at[s, lo:hi], here.up(sign))
    yield
    terms = mine(0)
    got.wait_recv()
    zsum[lo:hi] = add(*terms, box[6, lo:hi])


def plane_sum(snd, zsum, xbox, g_buf, here):
    copies = []
    for d in range(1, 16):
        to = wrap(here.g, d, 16)
        copies.append(snd.go(zsum.at[pl.ds(start_at(to), 3)], xbox.at[d], here.peer(d)))
    total = zsum[pl.ds(start_at(here.g), 3)].astype(F32)
    for d in range(1, 16):
        copies[d - 1].wait_recv()
        total = total + xbox[d].astype(F32)
    g_buf[here.y, here.x, here.z] = total.astype(BF16)
    own = g_buf.at[here.y, here.x, here.z]
    return [snd.go(own, own, here.up(d)) for d in range(1, 8)]


def z_at(buf, here, lo, hi, y_first):
    mid = (lo + hi) // 2
    parts = {None: (lo, hi), 0: (lo, mid), 1: (mid, hi)}

    def at(da, db, part):
        dy, dx = (da, db) if y_first else (db, da)
        a, b = parts[part]
        return buf.at[wrap(here.y, dy, 4), wrap(here.x, dx, 4), a:b]
    return at


def weight_out(snd, g_buf, g_sib, here):
    cores = []
    streams = []
    for lo, hi, yf in ((0, 4, False), (4, 8, True)):
        at = z_at(g_buf, here, lo, hi, yf)
        to = z_at(g_sib, here, lo, hi, yf)
        streams.append(gather_stream(
            snd, at, plane_dev(here, yf),
            lambda da, db, at=at, to=to: cores.append(snd.go(at(da, db, None), to(da, db, None), here.sibling()))))
    interleave(streams)
    for c in cores:
        c.wait_recv()


def unpack(g_buf, g_sib, flat, here, g0, g1, g2):
    for buf, base in ((g_buf, here.c * TILES), (g_sib, (1 - here.c) * TILES)):
        for g in range(16):
            for z in range(8):
                flat[pl.ds(base + (z * PIECE + start_at(g)), 3)] = buf[g // 4, g % 4, z]
    for c in range(5):
        g0[:, c * C : (c + 1) * C] = flat[c * 40 : c * 40 + 40].reshape(640, C).astype(F32)
    for i in range(2):
        for c in range(4):
            b = 200 + i * 128 + c * 32
            g1[i, :, c * C : (c + 1) * C] = flat[b : b + 32].reshape(512, C).astype(F32)
        for c in range(3):
            b = 456 + i * 72 + c * 24
            g2[i, :, c * C : (c + 1) * C] = flat[b : b + 24].reshape(384, C).astype(F32)


Z_STREAMS = ((1, 0, 10), (-1, 19, 29), (1, 10, 19), (-1, 29, 38))


def all_partners(here):
    return [here.sibling()] + [here.up(d) for d in range(1, 8)] + [here.peer(d) for d in range(1, 16)]


RCHUNKS = ((0, 9), (9, 16), (16, 25))


def reduce_kernel(chunks, p_out, p_grad, w_flat, out, grad, g0, g1, g2,
                  mid, t, r, q, t2, r2, sib, box, outbox, zsum, xbox, g_buf, g_sib, flat, send, recv):
    here = Place()
    greet(all_partners(here))
    snd = Sender(send, recv)
    copies = swap_cores(snd, w_flat, sib, here)
    seen = set()
    streams = [z_stream(snd, copies, seen, w_flat, sib, box, outbox, zsum, here, *z) for z in Z_STREAMS]
    for lo, hi in chunks:
        for i, (part, dst, yf) in enumerate(((p_out, out, True), (p_grad, grad, False))):
            streams.append(scatter_stream(snd, part, mid.at[i], t.at[i], r.at[i], q.at[i], t2.at[i], r2.at[i], dst, here, lo, hi, yf))
    interleave(streams)
    for c in plane_sum(snd, zsum, xbox, g_buf, here):
        c.wait_recv()
    weight_out(snd, g_buf, g_sib, here)
    snd.finish()
    unpack(g_buf, g_sib, flat, here, g0, g1, g2)


def reduce(p_out, p_grad, w_flat, chunks=RCHUNKS):
    v = pl.BlockSpec(memory_space=pltpu.VMEM)
    V = pltpu.VMEM
    n = 8 + 28 + 16 * len(chunks) + 15 + 7 + 2 * (20 + 16)
    o = jax.ShapeDtypeStruct((1, 16, W), BF16)
    return pl.pallas_call(
        functools.partial(reduce_kernel, chunks),
        out_shape=(o, o, jax.ShapeDtypeStruct((640, 640), F32), jax.ShapeDtypeStruct((2, 512, 512), F32),
                   jax.ShapeDtypeStruct((2, 384, 384), F32)),
        in_specs=[v] * 3, out_specs=(v,) * 5,
        scratch_shapes=[
            V((2, 2, 4, 16, W), BF16), V((2, 2, 4, 16, W), BF16), V((2, 2, 4, 16, W), BF16), V((2, 4, 16, W), BF16),
            V((2, 2, 16, W), BF16), V((2, 2, 16, W), BF16),
            V((TILES, 16, C), BF16), V((7, PIECE, 16, C), BF16), V((7, PIECE, 16, C), BF16), V((PIECE, 16, C), BF16),
            V((16, 3, 16, C), BF16), V((4, 4, 8, 3, 16, C), BF16), V((4, 4, 8, 3, 16, C), BF16), V((2 * TILES, 16, C), BF16),
            pltpu.SemaphoreType.DMA((n,)), pltpu.SemaphoreType.DMA((n,))],
        compiler_params=pltpu.CompilerParams(collective_id=1, has_side_effects=True, vmem_limit_bytes=56 * 2**20),
        name="reduce_all",
    )(p_out.reshape(4, 4, 16, W), p_grad.reshape(4, 4, 16, W), w_flat)


def per_device(node_feats, source, target, rotation, radial, edge_count, cotangent, weight_zero, weight_first, weight_second):
    feats, cots = gather(node_feats, cotangent)
    p_out, p_grad, flat = compute(
        edge_count, source, target, rotation[0], radial[0], feats, cots, weight_zero, weight_first, weight_second)
    return tuple(reduce(p_out, p_grad, flat))


def solution(mesh):
    edge = P("dp", "graph")
    node = P("dp", "graph", None)
    return jax.shard_map(
        per_device,
        mesh=mesh,
        in_specs=(node, edge, edge, P("dp", None, "graph"), node, edge, node, P(), P(), P()),
        out_specs=(node, node, P(), P(), P()),
        check_vma=False,
    )
```

```python
import functools, math
import jax, jax.numpy as jnp, numpy as np
from jax import lax
from jax.experimental import pallas as pl
from jax.experimental.pallas import tpu as pltpu
from jax.sharding import PartitionSpec as P

C = 128
E = 128
N = 256
W = 25 * C
F32, BF16 = jnp.float32, jnp.bfloat16
OFF = [0, 1, 10, 35, 84]


def dot(a, b):
    return lax.dot_general(a, b, (((1,), (0,)), ((), ())), preferred_element_type=F32)


def dot_nt(a, b):
    return lax.dot_general(a, b, (((1,), (1,)), ((), ())), preferred_element_type=F32)


def dot_tn(a, b):
    return lax.dot_general(a, b, (((0,), (0,)), ((), ())), preferred_element_type=F32)


def orders(l):
    top = min(l, 2)
    return range(-top, top + 1)


def kept(l):
    return sum(len(orders(q)) * (2 * q + 1) for q in range(l))


def prepare(src, dst, count, rot, oh_s, oh_d, oh_st, oh_dt, rot_t):
    node = lax.broadcasted_iota(jnp.int32, (N, E), 0)
    slot = lax.broadcasted_iota(jnp.int32, (N, E), 1)
    s = (node == src).astype(F32)
    d = ((node == dst) & (slot < count)).astype(F32)
    oh_st[...] = s.astype(BF16)
    oh_dt[...] = d.astype(BF16)
    oh_s[...] = s.T.astype(BF16)
    oh_d[...] = d.T.astype(BF16)
    eye = (lax.broadcasted_iota(jnp.int32, (E, E), 0) == lax.broadcasted_iota(jnp.int32, (E, E), 1)).astype(BF16)
    k = lax.broadcasted_iota(jnp.int32, (1, 165), 1)
    scale = jnp.ones((1, 165), F32)
    for l in range(1, 5):
        scale = jnp.where(k >= OFF[l], 1.0 / math.sqrt(2 * l + 1), scale)
    rot_t[:, :165] = dot_nt(eye, rot) * scale


def group_slot(l, m):
    return abs(m), (E if m < 0 else 0), (l - abs(m)) * C


PARTS = (1, 1, 1, 2, 2)


def loop_parts(step, parts):
    for p in range(parts):
        if p:
            yield
        pl.loop(p * 8 // parts, (p + 1) * 8 // parts)(step)


def rotate_in(l, feats, cots, oh_s, oh_d, rad, rot_t, x_buf, u_buf, wide, act, ups, ups_s):
    size = 2 * l + 1
    cols = slice(l * l * C, (l + 1) * (l + 1) * C)
    x_buf[:, : size * C] = dot(oh_s[...], feats[:, :, :, cols].reshape(N, size * C))
    u_buf[:, : size * C] = dot(oh_d[...], cots[:, :, :, cols].reshape(N, size * C))

    def step(b):
        r = pl.multiple_of(b * 16, 16)
        rows = pl.ds(r, 16)
        rt = rot_t[rows, :]
        xs = [x_buf[rows, j * C : (j + 1) * C] for j in range(size)]
        us = [u_buf[rows, j * C : (j + 1) * C] for j in range(size)]
        rd = rad[rows, l * C : (l + 1) * C].astype(F32)
        at = kept(l)
        for m in orders(l):
            a = u = None
            for j in range(size):
                k = OFF[l] + (m + l) * size + j
                w = jnp.broadcast_to(rt[:, k : k + 1], (16, C))
                wide[at, rows, :] = w
                at += 1
                a = w * xs[j] if a is None else a + w * xs[j]
                u = w * us[j] if u is None else u + w * us[j]
            g, ro, co = group_slot(l, m)
            here = pl.ds(r + ro, 16)
            cols = slice(co, co + C)
            act[g][here, cols] = (a * rd).astype(BF16)
            ub = u.astype(BF16)
            ups[g][here, cols] = ub
            if g:
                there = pl.ds(r + E - ro, 16)
                ups_s[g][there, cols] = ub if m < 0 else -ub

    yield from loop_parts(step, PARTS[l])


def plane(act, ups, ws, msg, back):
    msg[0][...] = dot(act[0][...], ws[0][...])
    back[0][...] = dot_nt(ups[0][...], ws[0][...])
    for g in (1, 2):
        a = act[g][...]
        y0 = dot(a, ws[g][0])
        y1 = dot(a, ws[g][1])
        msg[g][:E, :] = y0[:E] - y1[E:]
        msg[g][E:, :] = y0[E:] + y1[:E]
        u = ups[g][...]
        z0 = dot_nt(u, ws[g][0])
        z1 = dot_nt(u, ws[g][1])
        back[g][:E, :] = z0[:E] + z1[E:]
        back[g][E:, :] = z0[E:] - z1[:E]


def rotate_out(l, msg, back, rad, wide, oh_st, oh_dt, m_buf, e_buf, out, grad):
    size = 2 * l + 1

    def step(b):
        r = pl.multiple_of(b * 16, 16)
        rows = pl.ds(r, 16)
        rd = rad[rows, l * C : (l + 1) * C].astype(F32)
        ms, bs = [], []
        for m in orders(l):
            g, ro, co = group_slot(l, m)
            here = pl.ds(r + ro, 16)
            ms.append(msg[g][here, co : co + C])
            bs.append(back[g][here, co : co + C] * rd)
        n = len(ms)
        for i in range(size):
            a = u = None
            for j in range(n):
                w = wide[kept(l) + j * size + i, rows, :]
                a = w * ms[j] if a is None else a + w * ms[j]
                u = w * bs[j] if u is None else u + w * bs[j]
            m_buf[rows, i * C : (i + 1) * C] = a.astype(BF16)
            e_buf[rows, i * C : (i + 1) * C] = u.astype(BF16)

    yield from loop_parts(step, PARTS[l])
    cols = slice(l * l * C, (l + 1) * (l + 1) * C)
    shape = (4, 4, 16, size * C)
    out[:, :, :, cols] = dot(oh_dt[...], m_buf[:, : size * C]).astype(BF16).reshape(shape)
    grad[:, :, :, cols] = dot(oh_st[...], e_buf[:, : size * C]).astype(BF16).reshape(shape)


def weight_grads(act, ups, ups_s, flat):
    scale = 1.0 / math.sqrt(32768)
    at = 0
    for g in range(3):
        left = act[g][...].T
        for right in (ups, ups_s)[: 1 if g == 0 else 2]:
            total = (dot(left, right[g][...]) * scale).astype(BF16)
            rows = total.shape[0]
            for c in range(rows // C):
                flat[at : at + rows // 16] = total[:, c * C : (c + 1) * C].reshape(rows // 16, 16, C)
                at += rows // 16
    flat[600:608] = jnp.zeros((8, 16, C), BF16)


MESH = pl.DeviceIdType.MESH
TILES = 304
HALVES = ((0, 10), (160, 9))


def start_at(z):
    return lax.div(z * 16, 7) if not isinstance(z, int) else z * 16 // 7


def wrap(p, d, n):
    return lax.rem(p + (d % n), n)


class Place:
    def __init__(self):
        g, p = lax.axis_index("graph"), lax.axis_index("dp")
        self.g, self.p = g, p
        self.y, self.x = lax.div(g, 4), lax.rem(g, 4)
        self.z, self.c = lax.div(p, 2), lax.rem(p, 2)

    def plane(self, dy, dx):
        return (self.p, wrap(self.y, dy, 4) * 4 + wrap(self.x, dx, 4))

    def peer(self, d):
        return (self.p, wrap(self.g, d, 16))

    def up(self, d):
        return (wrap(self.z, d, 8) * 2 + self.c, self.g)

    def sibling(self):
        return (self.z * 2 + 1 - self.c, self.g)


class Sender:
    def __init__(self, send, recv):
        self.send, self.recv, self.next, self.open, self.most = send, recv, 0, [], 0

    def go(self, src, dst, to):
        c = pltpu.make_async_remote_copy(src_ref=src, dst_ref=dst, send_sem=self.send.at[len(self.open)],
                                         recv_sem=self.recv.at[self.next], device_id=to, device_id_type=MESH)
        self.next += 1
        self.open.append(c)
        c.start()
        return c

    def drain(self):
        for c in self.open:
            c.wait_send()
        self.open = []


class Runner:
    def __init__(self):
        self.active = []

    def add(self, stream, delay=0):
        self.active.append([stream, delay])
        return stream

    def run(self):
        while self.active:
            for entry in list(self.active):
                if entry[1] > 0:
                    entry[1] -= 1
                    continue
                try:
                    next(entry[0])
                except StopIteration:
                    self.active.remove(entry)


def gather_stream(snd, at, dev):
    def spread(da):
        return [snd.go(at(da, 0, None), at(da, 0, None), dev(0, s)) for s in (1, -1)]

    def relay(da, got):
        for k, s in enumerate((1, -1)):
            yield
            got[k].wait_recv()
            last.append(snd.go(at(da, -s, k), at(da, -s, k), dev(0, s)))

    last = []
    first = {-s: snd.go(at(0, 0, None), at(0, 0, None), dev(s, 0)) for s in (1, -1)}
    second = {0: spread(0)}
    first[2] = snd.go(at(0, 0, None), at(0, 0, None), dev(2, 0))
    for da in (-1, 1):
        yield
        first[da].wait_recv()
        second[da] = spread(da)
    yield from relay(0, second[0])
    yield
    first[2].wait_recv()
    second[2] = spread(2)
    for da in (-1, 1, 2):
        yield from relay(da, second[da])
    for f in last:
        yield
        f.wait_recv()


def col_at(buf, here, lo, hi, y_first):
    mid = (lo + hi) // 2
    parts = {None: (lo, hi), 0: (lo, mid), 1: (mid, hi)}

    def at(da, db, part):
        dy, dx = (da, db) if y_first else (db, da)
        a, b = parts[part]
        return buf.at[wrap(here.y, dy, 4), wrap(here.x, dx, 4), :, a * C : b * C]
    return at


def plane_dev(here, y_first):
    return (lambda da, db: here.plane(da, db)) if y_first else (lambda da, db: here.plane(db, da))


def add(*xs):
    t = xs[0].astype(F32)
    for x in xs[1:]:
        t = t + x.astype(F32)
    return t.astype(BF16)


def scatter_stream(snd, part, mid, t, r, q, r2, out, here, lo, hi, y_first):
    cm = (lo + hi) // 2
    full, halves = slice(lo * C, hi * C), (slice(lo * C, cm * C), slice(cm * C, hi * C))
    a, b = (here.y, here.x) if y_first else (here.x, here.y)
    dev = plane_dev(here, y_first)

    def row(da, cols):
        i = wrap(a, da, 4)
        return part.at[i, :, :, cols] if y_first else part.at[:, i, :, cols]

    got = [snd.go(row(2, halves[k]), t.at[k, :, :, halves[k]], dev(s, 0)) for k, s in enumerate((1, -1))]
    sent = []
    for k, s in enumerate((1, -1)):
        yield
        got[k].wait_recv()
        mid[k, :, :, halves[k]] = add(row(s, halves[k])[...], t[k, :, :, halves[k]])
        mid[k, :, :, halves[1 - k]] = row(s, halves[1 - k])[...]
        sent.append(snd.go(mid.at[k, :, :, full], r.at[k, :, :, full], dev(s, 0)))
    yield
    sent[0].wait_recv()
    sent[1].wait_recv()
    q[:, :, full] = add(row(0, full)[...], r[0, :, :, full], r[1, :, :, full])
    sent = []
    for k, s in enumerate((2, 1, -1)):
        sent.append(snd.go(q.at[wrap(b, s, 4), :, full], r2.at[k, :, full], dev(0, s)))
    yield
    for c in sent:
        c.wait_recv()
    out[:, full] = add(q[b, :, full], *(r2[k, :, full] for k in range(3)))


def block(ref, base, size, a, b, count=1):
    return ref.at[pl.ds(base + (a * 4 + b) * size, size * count)]


def weight_start(snd, flat, sib, here):
    other = (1 - here.c) * TILES
    copies = {}
    for da in (2, 1, -1, 0):
        for part, (off, size) in enumerate(HALVES):
            a = wrap(here.y if part == 0 else here.x, da, 4)
            copies[part, da] = snd.go(block(flat, other + off, size, a, 0, 4), block(sib, off, size, a, 0, 4), here.sibling())
    return copies


def weight_plane(snd, copies, part, flat, sib, hsum, tbox, qsum, t2box, zin, here):
    off, size = HALVES[part]
    y_first = part == 0
    a, b = (here.y, here.x) if y_first else (here.x, here.y)
    dev = plane_dev(here, y_first)
    own = here.c * TILES
    sent = []
    for k, da in enumerate((2, 1, -1)):
        copies[part, da].wait_recv()
        i = wrap(a, da, 4)
        block(hsum, off, size, i, 0, 4)[...] = add(block(flat, own + off, size, i, 0, 4)[...], block(sib, off, size, i, 0, 4)[...])
        sent.append(snd.go(block(hsum, off, size, i, 0, 4), tbox.at[k, off // 4 : off // 4 + 4 * size], dev(da, 0)))
    copies[part, 0].wait_recv()
    yield
    for c in sent:
        c.wait_recv()
    rows = slice(off // 4, off // 4 + 4 * size)
    qsum[rows] = add(block(flat, own + off, size, a, 0, 4)[...], block(sib, off, size, a, 0, 4)[...], *(tbox[k, rows] for k in range(3)))
    sent = []
    for k, db in enumerate((2, 1, -1)):
        i = wrap(b, db, 4)
        sent.append(snd.go(qsum.at[pl.ds(off // 4 + i * size, size)], t2box.at[k, off // 16 : off // 16 + size], dev(0, db)))
    yield
    for c in sent:
        c.wait_recv()
    rows = slice(off // 16, off // 16 + size)
    zin[rows] = add(qsum[pl.ds(off // 4 + b * size, size)], *(t2box[k, rows] for k in range(3)))


def weight_z(snd, zin, zbox, zall, zout, res, here):
    copies = [snd.go(zin.at[pl.ds(start_at(wrap(here.z, d, 8)), 3)], zbox.at[d], here.up(d)) for d in range(1, 8)]
    yield
    total = zin[pl.ds(start_at(here.z), 3)].astype(F32)
    for d in range(1, 8):
        copies[d - 1].wait_recv()
        total = total + zbox[d].astype(F32)
    zall[here.z] = total.astype(BF16)
    copies = [snd.go(zall.at[here.z], zall.at[here.z], here.up(d)) for d in range(1, 8)]
    yield
    for c in copies:
        c.wait_recv()
    for z in range(8):
        zout[start_at(z) : start_at(z) + 3] = zall[z]
    for part, (off, size) in enumerate(HALVES):
        a, b = (here.y, here.x) if part == 0 else (here.x, here.y)
        block(res, here.c * TILES + off, size, a, b)[...] = zout[off // 16 : off // 16 + size]


def weight_spread(snd, part, res, here, cores):
    off, size = HALVES[part]
    y_first = part == 0
    a, b = (here.y, here.x) if y_first else (here.x, here.y)
    dev = plane_dev(here, y_first)

    def at(da, db):
        return block(res, here.c * TILES + off, size, wrap(a, da, 4), wrap(b, db, 4))

    def to_core(da):
        row = block(res, here.c * TILES + off, size, wrap(a, da, 4), 0, 4)
        cores.append(snd.go(row, row, here.sibling()))

    first = {-d % 4: snd.go(at(0, 0), at(0, 0), dev(d, 0)) for d in (1, -1, 2)}
    second = {}
    for db in (1, -1, 2):
        second[0, -db % 4] = snd.go(at(0, 0), at(0, 0), dev(0, db))
    for da in (1, 3, 2):
        yield
        first[da].wait_recv()
        for db in (1, -1, 2):
            second[da, -db % 4] = snd.go(at(da, 0), at(da, 0), dev(0, db))
    for da in (0, 1, 3, 2):
        yield
        for db in (1, 3, 2):
            second[da, db].wait_recv()
        to_core(da)


CHUNKS = (((0, 1, 2), 0), ((3,), 2), ((4,), 4))
RCHUNKS = ((4,), (3,), (0, 1, 2))
ORDER = "wnnwnwn"


def bounds(degrees):
    return degrees[0] ** 2, (degrees[-1] + 1) ** 2


def block_kernel(count, src_in, dst_in, rot_in, rad_in, f_in, c_in, w0_in, w1_in, w2_in, out, grad, res,
                 src, dst, rot, rad, f_buf, c_buf, oh_s, oh_d, oh_st, oh_dt, rot_t, x_buf, u_buf, wide, a0, a1, a2, u0, u1, u2, v1, v2,
                 m0, m1, m2, b0, b1, b2, mb, eb, w0, w1, w2, p_out, p_grad, mid, t, r, q, r2,
                 flat, sib, hsum, tbox, qsum, t2box, zin, zbox, zall, zout, send, recv, w_sem):
    here = Place()
    loads = [pltpu.make_async_copy(i, o, w_sem.at[k]) for k, (i, o) in enumerate((
        (f_in.at[0], f_buf.at[here.y, here.x]), (c_in.at[0], c_buf.at[here.y, here.x]), (src_in, src), (dst_in, dst),
        (rot_in, rot), (rad_in, rad), (w0_in, w0), (w1_in, w1), (w2_in, w2)))]
    for c in loads:
        c.start()
    partners = [here.sibling()] + [here.up(d) for d in range(1, 8)] + [here.peer(d) for d in range(1, 16)]
    barrier = pltpu.get_barrier_semaphore()
    for d in partners:
        pl.semaphore_signal(barrier, inc=1, device_id=d, device_id_type=MESH)
    for c in loads[:5]:
        c.wait()
    prepare(src[...], dst[...], count[0, 0], rot[...], oh_s, oh_d, oh_st, oh_dt, rot_t)
    pl.semaphore_wait(barrier, len(partners))
    loads[5].wait()

    act, ups, ups_s = (a0, a1, a2), (u0, u1, u2), (None, v1, v2)
    ws, msg, back = (w0, w1, w2), (m0, m1, m2), (b0, b1, b2)
    snd = Sender(send, recv)
    run = Runner()

    def take_in(degrees, parts):
        for p in parts:
            yield from p
        for l in degrees:
            yield
            yield from rotate_in(l, f_buf, c_buf, oh_s, oh_d, rad, rot_t, x_buf, u_buf, wide, act, ups, ups_s)

    def both(lo, hi):
        f = gather_stream(snd, col_at(f_buf, here, lo, hi, False), plane_dev(here, False))
        c = gather_stream(snd, col_at(c_buf, here, lo, hi, True), plane_dev(here, True))
        live = [f, c]
        while live:
            for s in list(live):
                try:
                    next(s)
                except StopIteration:
                    live.remove(s)
            if live:
                yield

    starts = []
    for degrees, delay in CHUNKS:
        stream = both(*bounds(degrees))
        next(stream)
        run.add(take_in(degrees, [stream]), delay)
    run.run()

    weight_grads(act, ups, ups_s, flat)
    snd.drain()
    copies = weight_start(snd, flat, sib, here)

    def turns(streams):
        live = list(streams)
        while live:
            for s in list(live):
                try:
                    next(s)
                except StopIteration:
                    live.remove(s)
            yield

    def weights():
        yield from turns([weight_plane(snd, copies, p, flat, sib, hsum, tbox, qsum, t2box, zin, here) for p in range(2)])
        yield from weight_z(snd, zin, zbox, zall, zout, res, here)
        cores = []
        yield from turns([weight_spread(snd, p, res, here, cores) for p in range(2)])
        for c in cores:
            c.wait_recv()

    sums = weights()
    rows = []
    for c in loads[6:]:
        c.wait()
    plane(act, ups, ws, msg, back)
    for k, degrees in enumerate(RCHUNKS):
        for l in degrees:
            for _ in rotate_out(l, msg, back, rad, wide, oh_st, oh_dt, mb, eb, p_out, p_grad):
                pass
        lo, hi = bounds(degrees)
        for i, (part, dst_ref, yf) in enumerate(((p_out, out, True), (p_grad, grad, False))):
            rows.append(scatter_stream(snd, part, mid.at[i], t.at[i], r.at[i], q.at[i], r2.at[i], dst_ref, here, lo, hi, yf))
            next(rows[-1])
        if k == 0:
            next(sums)
    for step in ORDER:
        if step == "w":
            next(sums, None)
        else:
            for s in rows:
                next(s, None)
    for _ in sums:
        pass
    snd.drain()


def edge_block(count, src, dst, rot, rad, feats, cots, w0, w1, w2):
    v = pl.BlockSpec(memory_space=pltpu.VMEM)
    h = pl.BlockSpec(memory_space=pltpu.HBM)
    V = pltpu.VMEM
    rows = jax.ShapeDtypeStruct((16, W), BF16)
    n_send, n_recv = 114, 228
    return pl.pallas_call(
        block_kernel,
        out_shape=(rows, rows, jax.ShapeDtypeStruct((2 * TILES, 16, C), BF16)),
        in_specs=[pl.BlockSpec(memory_space=pltpu.SMEM)] + [h] * 9,
        out_specs=(v,) * 3,
        scratch_shapes=[
            V((1, E), jnp.int32), V((1, E), jnp.int32), V((165, E), BF16), V((E, 640), BF16),
            V((4, 4, 16, W), BF16), V((4, 4, 16, W), BF16),
            V((E, N), BF16), V((E, N), BF16), V((N, E), BF16), V((N, E), BF16), V((E, 256), F32),
            V((E, 9 * C), F32), V((E, 9 * C), F32), V((115, E, C), F32),
            V((E, 640), BF16), V((2 * E, 512), BF16), V((2 * E, 384), BF16),
            V((E, 640), BF16), V((2 * E, 512), BF16), V((2 * E, 384), BF16),
            V((2 * E, 512), BF16), V((2 * E, 384), BF16),
            V((E, 640), F32), V((2 * E, 512), F32), V((2 * E, 384), F32),
            V((E, 640), F32), V((2 * E, 512), F32), V((2 * E, 384), F32),
            V((E, 9 * C), BF16), V((E, 9 * C), BF16),
            V((640, 640), BF16), V((2, 512, 512), BF16), V((2, 384, 384), BF16),
            V((4, 4, 16, W), BF16), V((4, 4, 16, W), BF16),
            V((2, 2, 4, 16, W), BF16), V((2, 2, 4, 16, W), BF16), V((2, 2, 4, 16, W), BF16), V((2, 4, 16, W), BF16),
            V((2, 3, 16, W), BF16),
            V((2 * TILES, 16, C), BF16), V((TILES, 16, C), BF16), V((TILES, 16, C), BF16), V((3, 76, 16, C), BF16),
            V((76, 16, C), BF16), V((3, 19, 16, C), BF16), V((19, 16, C), BF16), V((8, 3, 16, C), BF16), V((8, 3, 16, C), BF16),
            V((19, 16, C), BF16),
            pltpu.SemaphoreType.DMA((n_send,)), pltpu.SemaphoreType.DMA((n_recv,)), pltpu.SemaphoreType.DMA((9,)),
        ],
        compiler_params=pltpu.CompilerParams(collective_id=0, has_side_effects=True, vmem_limit_bytes=60 * 2**20),
        name="edge_block",
    )(count, src, dst, rot, rad, feats, cots, w0, w1, w2)


def finish_kernel(rows_in, grad_in, flat, rows, grad, g0, g1, g2):
    rows[0] = rows_in[...]
    grad[0] = grad_in[...]
    for c in range(5):
        g0[:, c * C : (c + 1) * C] = flat[c * 40 : c * 40 + 40].reshape(640, C).astype(F32)
    for i in range(2):
        for c in range(4):
            b = 200 + i * 128 + c * 32
            g1[i, :, c * C : (c + 1) * C] = flat[b : b + 32].reshape(512, C).astype(F32)
        for c in range(3):
            b = 456 + i * 72 + c * 24
            g2[i, :, c * C : (c + 1) * C] = flat[b : b + 24].reshape(384, C).astype(F32)


def finish(rows, grad, flat):
    v = pl.BlockSpec(memory_space=pltpu.VMEM)
    o = jax.ShapeDtypeStruct((1, 16, W), BF16)
    return pl.pallas_call(
        finish_kernel,
        out_shape=(o, o, jax.ShapeDtypeStruct((640, 640), F32), jax.ShapeDtypeStruct((2, 512, 512), F32),
                   jax.ShapeDtypeStruct((2, 384, 384), F32)),
        in_specs=[v] * 3, out_specs=(v,) * 5,
        compiler_params=pltpu.CompilerParams(vmem_limit_bytes=60 * 2**20),
        name="finish",
    )(rows, grad, flat)


def per_device(node_feats, source, target, rotation, radial, edge_count, cotangent, weight_zero, weight_first, weight_second):
    rows, grad, flat = edge_block(
        edge_count, source, target, rotation[0], radial[0], node_feats, cotangent, weight_zero, weight_first, weight_second)
    return tuple(finish(rows, grad, flat))


def solution(mesh):
    edge = P("dp", "graph")
    node = P("dp", "graph", None)
    return jax.shard_map(
        per_device,
        mesh=mesh,
        in_specs=(node, edge, edge, P("dp", None, "graph"), node, edge, node, P(), P(), P()),
        out_specs=(node, node, P(), P(), P()),
        check_vma=False,
    )
```

```python
import functools, math
import jax, jax.numpy as jnp, numpy as np
from jax import lax
from jax.experimental import pallas as pl
from jax.experimental.pallas import tpu as pltpu
from jax.sharding import PartitionSpec as P

C = 128
E = 128
N = 256
W = 25 * C
F32, BF16 = jnp.float32, jnp.bfloat16
OFF = [0, 1, 10, 35, 84]


def dot(a, b):
    return lax.dot_general(a, b, (((1,), (0,)), ((), ())), preferred_element_type=F32)


def dot_nt(a, b):
    return lax.dot_general(a, b, (((1,), (1,)), ((), ())), preferred_element_type=F32)


def dot_tn(a, b):
    return lax.dot_general(a, b, (((0,), (0,)), ((), ())), preferred_element_type=F32)


def orders(l):
    top = min(l, 2)
    return range(-top, top + 1)


def kept(l):
    return sum(len(orders(q)) * (2 * q + 1) for q in range(l))


def prepare(src, dst, count, rot, oh_s, oh_d, oh_st, oh_dt, rot_t):
    node = lax.broadcasted_iota(jnp.int32, (N, E), 0)
    slot = lax.broadcasted_iota(jnp.int32, (N, E), 1)
    s = (node == src).astype(F32)
    d = ((node == dst) & (slot < count)).astype(F32)
    oh_st[...] = s.astype(BF16)
    oh_dt[...] = d.astype(BF16)
    oh_s[...] = s.T.astype(BF16)
    oh_d[...] = d.T.astype(BF16)
    eye = (lax.broadcasted_iota(jnp.int32, (E, E), 0) == lax.broadcasted_iota(jnp.int32, (E, E), 1)).astype(BF16)
    k = lax.broadcasted_iota(jnp.int32, (1, 165), 1)
    scale = jnp.ones((1, 165), F32)
    for l in range(1, 5):
        scale = jnp.where(k >= OFF[l], 1.0 / math.sqrt(2 * l + 1), scale)
    rot_t[:, :165] = dot_nt(eye, rot) * scale


def group_slot(l, m):
    return abs(m), (E if m < 0 else 0), (l - abs(m)) * C


PARTS = (1, 1, 1, 2, 2)


def loop_parts(step, parts):
    for p in range(parts):
        if p:
            yield
        pl.loop(p * 8 // parts, (p + 1) * 8 // parts)(step)


def rotate_in(l, feats, cots, oh_s, oh_d, rad, rot_t, x_buf, u_buf, wide, act, ups, ups_s):
    size = 2 * l + 1
    cols = slice(l * l * C, (l + 1) * (l + 1) * C)
    x_buf[:, : size * C] = dot(oh_s[...], feats[:, :, :, cols].reshape(N, size * C))
    u_buf[:, : size * C] = dot(oh_d[...], cots[:, :, :, cols].reshape(N, size * C))

    def step(b):
        r = pl.multiple_of(b * 16, 16)
        rows = pl.ds(r, 16)
        rt = rot_t[rows, :]
        xs = [x_buf[rows, j * C : (j + 1) * C] for j in range(size)]
        us = [u_buf[rows, j * C : (j + 1) * C] for j in range(size)]
        rd = rad[rows, l * C : (l + 1) * C].astype(F32)
        at = kept(l)
        for m in orders(l):
            a = u = None
            for j in range(size):
                k = OFF[l] + (m + l) * size + j
                w = jnp.broadcast_to(rt[:, k : k + 1], (16, C))
                wide[at, rows, :] = w
                at += 1
                a = w * xs[j] if a is None else a + w * xs[j]
                u = w * us[j] if u is None else u + w * us[j]
            g, ro, co = group_slot(l, m)
            here = pl.ds(r + ro, 16)
            cols = slice(co, co + C)
            act[g][here, cols] = (a * rd).astype(BF16)
            ub = u.astype(BF16)
            ups[g][here, cols] = ub
            if g:
                there = pl.ds(r + E - ro, 16)
                ups_s[g][there, cols] = ub if m < 0 else -ub

    yield from loop_parts(step, PARTS[l])


def plane(act, ups, ws, msg, back):
    msg[0][...] = dot(act[0][...], ws[0][...])
    back[0][...] = dot_nt(ups[0][...], ws[0][...])
    for g in (1, 2):
        a = act[g][...]
        y0 = dot(a, ws[g][0])
        y1 = dot(a, ws[g][1])
        msg[g][:E, :] = y0[:E] - y1[E:]
        msg[g][E:, :] = y0[E:] + y1[:E]
        u = ups[g][...]
        z0 = dot_nt(u, ws[g][0])
        z1 = dot_nt(u, ws[g][1])
        back[g][:E, :] = z0[:E] + z1[E:]
        back[g][E:, :] = z0[E:] - z1[:E]


def rotate_out(l, msg, back, rad, wide, oh_st, oh_dt, m_buf, e_buf, out, grad):
    size = 2 * l + 1

    def step(b):
        r = pl.multiple_of(b * 16, 16)
        rows = pl.ds(r, 16)
        rd = rad[rows, l * C : (l + 1) * C].astype(F32)
        ms, bs = [], []
        for m in orders(l):
            g, ro, co = group_slot(l, m)
            here = pl.ds(r + ro, 16)
            ms.append(msg[g][here, co : co + C])
            bs.append(back[g][here, co : co + C] * rd)
        n = len(ms)
        for i in range(size):
            a = u = None
            for j in range(n):
                w = wide[kept(l) + j * size + i, rows, :]
                a = w * ms[j] if a is None else a + w * ms[j]
                u = w * bs[j] if u is None else u + w * bs[j]
            m_buf[rows, i * C : (i + 1) * C] = a.astype(BF16)
            e_buf[rows, i * C : (i + 1) * C] = u.astype(BF16)

    yield from loop_parts(step, PARTS[l])
    cols = slice(l * l * C, (l + 1) * (l + 1) * C)
    shape = (4, 4, 16, size * C)
    out[:, :, :, cols] = dot(oh_dt[...], m_buf[:, : size * C]).astype(BF16).reshape(shape)
    grad[:, :, :, cols] = dot(oh_st[...], e_buf[:, : size * C]).astype(BF16).reshape(shape)


def weight_grads(act, ups, ups_s, flat):
    scale = 1.0 / math.sqrt(32768)
    at = 0
    for g in range(3):
        left = act[g][...].T
        for right in (ups, ups_s)[: 1 if g == 0 else 2]:
            total = (dot(left, right[g][...]) * scale).astype(BF16)
            rows = total.shape[0]
            for c in range(rows // C):
                flat[at : at + rows // 16] = total[:, c * C : (c + 1) * C].reshape(rows // 16, 16, C)
                at += rows // 16
    flat[600:608] = jnp.zeros((8, 16, C), BF16)


MESH = pl.DeviceIdType.MESH
TILES = 304
HALVES = ((0, 10), (160, 9))


def start_at(z):
    return lax.div(z * 16, 7) if not isinstance(z, int) else z * 16 // 7


def wrap(p, d, n):
    return lax.rem(p + (d % n), n)


class Place:
    def __init__(self):
        g, p = lax.axis_index("graph"), lax.axis_index("dp")
        self.g, self.p = g, p
        self.y, self.x = lax.div(g, 4), lax.rem(g, 4)
        self.z, self.c = lax.div(p, 2), lax.rem(p, 2)

    def plane(self, dy, dx):
        return (self.p, wrap(self.y, dy, 4) * 4 + wrap(self.x, dx, 4))

    def peer(self, d):
        return (self.p, wrap(self.g, d, 16))

    def up(self, d):
        return (wrap(self.z, d, 8) * 2 + self.c, self.g)

    def sibling(self):
        return (self.z * 2 + 1 - self.c, self.g)


class Sender:
    def __init__(self, send, recv):
        self.send, self.recv, self.next, self.open, self.most = send, recv, 0, [], 0

    def go(self, src, dst, to):
        c = pltpu.make_async_remote_copy(src_ref=src, dst_ref=dst, send_sem=self.send.at[len(self.open)],
                                         recv_sem=self.recv.at[self.next], device_id=to, device_id_type=MESH)
        self.next += 1
        self.open.append(c)
        c.start()
        return c

    def drain(self):
        for c in self.open:
            c.wait_send()
        self.open = []


class Runner:
    def __init__(self):
        self.active = []

    def add(self, stream, delay=0):
        self.active.append([stream, delay])
        return stream

    def run(self):
        while self.active:
            for entry in list(self.active):
                if entry[1] > 0:
                    entry[1] -= 1
                    continue
                try:
                    next(entry[0])
                except StopIteration:
                    self.active.remove(entry)


def gather_stream(snd, at, dev):
    def spread(da):
        return [snd.go(at(da, 0, None), at(da, 0, None), dev(0, s)) for s in (1, -1)]

    def relay(da, got):
        for k, s in enumerate((1, -1)):
            yield
            got[k].wait_recv()
            last.append(snd.go(at(da, -s, k), at(da, -s, k), dev(0, s)))

    last = []
    first = {-s: snd.go(at(0, 0, None), at(0, 0, None), dev(s, 0)) for s in (1, -1)}
    second = {0: spread(0)}
    first[2] = snd.go(at(0, 0, None), at(0, 0, None), dev(2, 0))
    for da in (-1, 1):
        yield
        first[da].wait_recv()
        second[da] = spread(da)
    yield from relay(0, second[0])
    yield
    first[2].wait_recv()
    second[2] = spread(2)
    for da in (-1, 1, 2):
        yield from relay(da, second[da])
    for f in last:
        yield
        f.wait_recv()


def col_at(buf, here, lo, hi, y_first):
    mid = (lo + hi) // 2
    parts = {None: (lo, hi), 0: (lo, mid), 1: (mid, hi)}

    def at(da, db, part):
        dy, dx = (da, db) if y_first else (db, da)
        a, b = parts[part]
        return buf.at[wrap(here.y, dy, 4), wrap(here.x, dx, 4), :, a * C : b * C]
    return at


def plane_dev(here, y_first):
    return (lambda da, db: here.plane(da, db)) if y_first else (lambda da, db: here.plane(db, da))


def add(*xs):
    t = xs[0].astype(F32)
    for x in xs[1:]:
        t = t + x.astype(F32)
    return t.astype(BF16)


def scatter_stream(snd, part, mid, t, r, q, r2, out, here, lo, hi, y_first):
    cm = (lo + hi) // 2
    full, halves = slice(lo * C, hi * C), (slice(lo * C, cm * C), slice(cm * C, hi * C))
    a, b = (here.y, here.x) if y_first else (here.x, here.y)
    dev = plane_dev(here, y_first)

    def row(da, cols):
        i = wrap(a, da, 4)
        return part.at[i, :, :, cols] if y_first else part.at[:, i, :, cols]

    got = [snd.go(row(2, halves[k]), t.at[k, :, :, halves[k]], dev(s, 0)) for k, s in enumerate((1, -1))]
    sent = []
    for k, s in enumerate((1, -1)):
        yield
        got[k].wait_recv()
        mid[k, :, :, halves[k]] = add(row(s, halves[k])[...], t[k, :, :, halves[k]])
        mid[k, :, :, halves[1 - k]] = row(s, halves[1 - k])[...]
        sent.append(snd.go(mid.at[k, :, :, full], r.at[k, :, :, full], dev(s, 0)))
    yield
    sent[0].wait_recv()
    sent[1].wait_recv()
    q[:, :, full] = add(row(0, full)[...], r[0, :, :, full], r[1, :, :, full])
    sent = []
    for k, s in enumerate((2, 1, -1)):
        sent.append(snd.go(q.at[wrap(b, s, 4), :, full], r2.at[k, :, full], dev(0, s)))
    yield
    for c in sent:
        c.wait_recv()
    out[:, full] = add(q[b, :, full], *(r2[k, :, full] for k in range(3)))


def block(ref, base, size, a, b, count=1):
    return ref.at[pl.ds(base + (a * 4 + b) * size, size * count)]


def weight_start(snd, flat, sib, here):
    other = (1 - here.c) * TILES
    copies = {}
    for da in (2, 1, -1, 0):
        for part, (off, size) in enumerate(HALVES):
            a = wrap(here.y if part == 0 else here.x, da, 4)
            copies[part, da] = snd.go(block(flat, other + off, size, a, 0, 4), block(sib, off, size, a, 0, 4), here.sibling())
    return copies


def weight_plane(snd, copies, part, flat, sib, hsum, tbox, qsum, t2box, zin, here):
    off, size = HALVES[part]
    y_first = part == 0
    a, b = (here.y, here.x) if y_first else (here.x, here.y)
    dev = plane_dev(here, y_first)
    own = here.c * TILES
    sent = []
    for k, da in enumerate((2, 1, -1)):
        copies[part, da].wait_recv()
        i = wrap(a, da, 4)
        block(hsum, off, size, i, 0, 4)[...] = add(block(flat, own + off, size, i, 0, 4)[...], block(sib, off, size, i, 0, 4)[...])
        sent.append(snd.go(block(hsum, off, size, i, 0, 4), tbox.at[k, off // 4 : off // 4 + 4 * size], dev(da, 0)))
    copies[part, 0].wait_recv()
    yield
    for c in sent:
        c.wait_recv()
    rows = slice(off // 4, off // 4 + 4 * size)
    qsum[rows] = add(block(flat, own + off, size, a, 0, 4)[...], block(sib, off, size, a, 0, 4)[...], *(tbox[k, rows] for k in range(3)))
    sent = []
    for k, db in enumerate((2, 1, -1)):
        i = wrap(b, db, 4)
        sent.append(snd.go(qsum.at[pl.ds(off // 4 + i * size, size)], t2box.at[k, off // 16 : off // 16 + size], dev(0, db)))
    yield
    for c in sent:
        c.wait_recv()
    rows = slice(off // 16, off // 16 + size)
    zin[rows] = add(qsum[pl.ds(off // 4 + b * size, size)], *(t2box[k, rows] for k in range(3)))


def weight_z(snd, zin, zbox, zall, zout, res, here):
    copies = [snd.go(zin.at[pl.ds(start_at(wrap(here.z, d, 8)), 3)], zbox.at[d], here.up(d)) for d in range(1, 8)]
    yield
    total = zin[pl.ds(start_at(here.z), 3)].astype(F32)
    for d in range(1, 8):
        copies[d - 1].wait_recv()
        total = total + zbox[d].astype(F32)
    zall[here.z] = total.astype(BF16)
    copies = [snd.go(zall.at[here.z], zall.at[here.z], here.up(d)) for d in range(1, 8)]
    yield
    for c in copies:
        c.wait_recv()
    for z in range(8):
        zout[start_at(z) : start_at(z) + 3] = zall[z]
    for part, (off, size) in enumerate(HALVES):
        a, b = (here.y, here.x) if part == 0 else (here.x, here.y)
        block(res, here.c * TILES + off, size, a, b)[...] = zout[off // 16 : off // 16 + size]


def weight_spread(snd, part, res, here, cores):
    off, size = HALVES[part]
    y_first = part == 0
    a, b = (here.y, here.x) if y_first else (here.x, here.y)
    dev = plane_dev(here, y_first)

    def at(da, db):
        return block(res, here.c * TILES + off, size, wrap(a, da, 4), wrap(b, db, 4))

    def to_core(da):
        row = block(res, here.c * TILES + off, size, wrap(a, da, 4), 0, 4)
        cores.append(snd.go(row, row, here.sibling()))

    first = {-d % 4: snd.go(at(0, 0), at(0, 0), dev(d, 0)) for d in (1, -1, 2)}
    second = {}
    for db in (1, -1, 2):
        second[0, -db % 4] = snd.go(at(0, 0), at(0, 0), dev(0, db))
    for da in (1, 3, 2):
        yield
        first[da].wait_recv()
        for db in (1, -1, 2):
            second[da, -db % 4] = snd.go(at(da, 0), at(da, 0), dev(0, db))
    for da in (0, 1, 3, 2):
        yield
        for db in (1, 3, 2):
            second[da, db].wait_recv()
        to_core(da)


CHUNKS = (((0, 1, 2), 0), ((3,), 2), ((4,), 4))
RCHUNKS = ((4,), (3,), (0, 1, 2))
ORDER = "wnnwnwn"
FIRST = 1


def bounds(degrees):
    return degrees[0] ** 2, (degrees[-1] + 1) ** 2


def block_kernel(count, src_in, dst_in, rot_in, rad_in, f_in, c_in, w0_in, w1_in, w2_in, out, grad, res,
                 src, dst, rot, rad, f_buf, c_buf, oh_s, oh_d, oh_st, oh_dt, rot_t, x_buf, u_buf, wide, a0, a1, a2, u0, u1, u2, v1, v2,
                 m0, m1, m2, b0, b1, b2, mb, eb, w0, w1, w2, p_out, p_grad, mid, t, r, q, r2,
                 flat, sib, hsum, tbox, qsum, t2box, zin, zbox, zall, zout, send, recv, w_sem):
    here = Place()
    loads = [pltpu.make_async_copy(i, o, w_sem.at[k]) for k, (i, o) in enumerate((
        (f_in.at[0], f_buf.at[here.y, here.x]), (c_in.at[0], c_buf.at[here.y, here.x]), (src_in, src), (dst_in, dst),
        (rot_in, rot), (rad_in, rad), (w0_in, w0), (w1_in, w1), (w2_in, w2)))]
    for c in loads:
        c.start()
    partners = [here.sibling()] + [here.up(d) for d in range(1, 8)] + [
        here.plane(*d) for d in ((0, 1), (0, -1), (0, 2), (1, 0), (-1, 0), (2, 0))]
    barrier = pltpu.get_barrier_semaphore()
    for d in partners:
        pl.semaphore_signal(barrier, inc=1, device_id=d, device_id_type=MESH)
    for c in loads[:5]:
        c.wait()
    prepare(src[...], dst[...], count[0, 0], rot[...], oh_s, oh_d, oh_st, oh_dt, rot_t)
    pl.semaphore_wait(barrier, len(partners))
    loads[5].wait()

    act, ups, ups_s = (a0, a1, a2), (u0, u1, u2), (None, v1, v2)
    ws, msg, back = (w0, w1, w2), (m0, m1, m2), (b0, b1, b2)
    snd = Sender(send, recv)
    run = Runner()

    def take_in(degrees, parts):
        for p in parts:
            yield from p
        for l in degrees:
            yield
            yield from rotate_in(l, f_buf, c_buf, oh_s, oh_d, rad, rot_t, x_buf, u_buf, wide, act, ups, ups_s)

    def both(lo, hi):
        f = gather_stream(snd, col_at(f_buf, here, lo, hi, False), plane_dev(here, False))
        c = gather_stream(snd, col_at(c_buf, here, lo, hi, True), plane_dev(here, True))
        live = [f, c]
        while live:
            for s in list(live):
                try:
                    next(s)
                except StopIteration:
                    live.remove(s)
            if live:
                yield

    starts = []
    for degrees, delay in CHUNKS:
        stream = both(*bounds(degrees))
        next(stream)
        run.add(take_in(degrees, [stream]), delay)
    run.run()

    weight_grads(act, ups, ups_s, flat)
    snd.drain()
    copies = weight_start(snd, flat, sib, here)

    def turns(streams):
        live = list(streams)
        while live:
            for s in list(live):
                try:
                    next(s)
                except StopIteration:
                    live.remove(s)
            yield

    def weights():
        yield from turns([weight_plane(snd, copies, p, flat, sib, hsum, tbox, qsum, t2box, zin, here) for p in range(2)])
        yield from weight_z(snd, zin, zbox, zall, zout, res, here)
        cores = []
        yield from turns([weight_spread(snd, p, res, here, cores) for p in range(2)])
        for c in cores:
            c.wait_recv()

    sums = weights()
    rows = []
    for c in loads[6:]:
        c.wait()
    plane(act, ups, ws, msg, back)
    for k, degrees in enumerate(RCHUNKS):
        if k == FIRST:
            next(sums)
        for l in degrees:
            for _ in rotate_out(l, msg, back, rad, wide, oh_st, oh_dt, mb, eb, p_out, p_grad):
                pass
        lo, hi = bounds(degrees)
        for i, (part, dst_ref, yf) in enumerate(((p_out, out, True), (p_grad, grad, False))):
            rows.append(scatter_stream(snd, part, mid.at[i], t.at[i], r.at[i], q.at[i], r2.at[i], dst_ref, here, lo, hi, yf))
            next(rows[-1])
    for step in ORDER:
        if step == "w":
            next(sums, None)
        else:
            for s in rows:
                next(s, None)
    for _ in sums:
        pass
    snd.drain()


def edge_block(count, src, dst, rot, rad, feats, cots, w0, w1, w2):
    v = pl.BlockSpec(memory_space=pltpu.VMEM)
    h = pl.BlockSpec(memory_space=pltpu.HBM)
    V = pltpu.VMEM
    rows = jax.ShapeDtypeStruct((16, W), BF16)
    n_send, n_recv = 114, 228
    return pl.pallas_call(
        block_kernel,
        out_shape=(rows, rows, jax.ShapeDtypeStruct((2 * TILES, 16, C), BF16)),
        in_specs=[pl.BlockSpec(memory_space=pltpu.SMEM)] + [h] * 9,
        out_specs=(v,) * 3,
        scratch_shapes=[
            V((1, E), jnp.int32), V((1, E), jnp.int32), V((165, E), BF16), V((E, 640), BF16),
            V((4, 4, 16, W), BF16), V((4, 4, 16, W), BF16),
            V((E, N), BF16), V((E, N), BF16), V((N, E), BF16), V((N, E), BF16), V((E, 256), F32),
            V((E, 9 * C), F32), V((E, 9 * C), F32), V((115, E, C), F32),
            V((E, 640), BF16), V((2 * E, 512), BF16), V((2 * E, 384), BF16),
            V((E, 640), BF16), V((2 * E, 512), BF16), V((2 * E, 384), BF16),
            V((2 * E, 512), BF16), V((2 * E, 384), BF16),
            V((E, 640), F32), V((2 * E, 512), F32), V((2 * E, 384), F32),
            V((E, 640), F32), V((2 * E, 512), F32), V((2 * E, 384), F32),
            V((E, 9 * C), BF16), V((E, 9 * C), BF16),
            V((640, 640), BF16), V((2, 512, 512), BF16), V((2, 384, 384), BF16),
            V((4, 4, 16, W), BF16), V((4, 4, 16, W), BF16),
            V((2, 2, 4, 16, W), BF16), V((2, 2, 4, 16, W), BF16), V((2, 2, 4, 16, W), BF16), V((2, 4, 16, W), BF16),
            V((2, 3, 16, W), BF16),
            V((2 * TILES, 16, C), BF16), V((TILES, 16, C), BF16), V((TILES, 16, C), BF16), V((3, 76, 16, C), BF16),
            V((76, 16, C), BF16), V((3, 19, 16, C), BF16), V((19, 16, C), BF16), V((8, 3, 16, C), BF16), V((8, 3, 16, C), BF16),
            V((19, 16, C), BF16),
            pltpu.SemaphoreType.DMA((n_send,)), pltpu.SemaphoreType.DMA((n_recv,)), pltpu.SemaphoreType.DMA((9,)),
        ],
        compiler_params=pltpu.CompilerParams(collective_id=0, has_side_effects=True, vmem_limit_bytes=60 * 2**20),
        name="edge_block",
    )(count, src, dst, rot, rad, feats, cots, w0, w1, w2)


def finish_kernel(rows_in, grad_in, flat_in, rows, grad, g0_out, g1_out, g2_out, flat, g0, g1, g2, sems):
    parts = ((0, 200), (200, 256), (456, 144))
    ends = []
    loads = [pltpu.make_async_copy(flat_in.at[b : b + n], flat.at[b : b + n], sems.at[k]) for k, (b, n) in enumerate(parts)]
    for c in loads:
        c.start()
    rows[0] = rows_in[...]
    grad[0] = grad_in[...]

    def send(k, src, dst):
        c = pltpu.make_async_copy(src, dst, sems.at[3 + k])
        c.start()
        ends.append(c)

    loads[0].wait()
    for c in range(5):
        g0[:, c * C : (c + 1) * C] = flat[c * 40 : c * 40 + 40].reshape(640, C).astype(F32)
    send(0, g0, g0_out)
    for k, (width, g, g_out) in enumerate(((4, g1, g1_out), (3, g2, g2_out))):
        loads[k + 1].wait()
        at = parts[k + 1][0]
        for i in range(2):
            for c in range(width):
                g[i, :, c * C : (c + 1) * C] = flat[at : at + 8 * width].reshape(width * C, C).astype(F32)
                at += 8 * width
            send(1 + 2 * k + i, g.at[i], g_out.at[i])
    for c in ends:
        c.wait()


def finish(rows, grad, flat):
    h = pl.BlockSpec(memory_space=pltpu.HBM)
    v = pl.BlockSpec(memory_space=pltpu.VMEM)
    V = pltpu.VMEM
    o = jax.ShapeDtypeStruct((1, 16, W), BF16)
    shapes = ((640, 640), (2, 512, 512), (2, 384, 384))
    return pl.pallas_call(
        finish_kernel,
        out_shape=(o, o) + tuple(jax.ShapeDtypeStruct(s, F32) for s in shapes),
        in_specs=[v, v, h], out_specs=(v, v, h, h, h),
        scratch_shapes=[V((2 * TILES, 16, C), BF16)] + [V(s, F32) for s in shapes] + [pltpu.SemaphoreType.DMA((8,))],
        compiler_params=pltpu.CompilerParams(vmem_limit_bytes=60 * 2**20),
        name="finish",
    )(rows, grad, flat)


def per_device(node_feats, source, target, rotation, radial, edge_count, cotangent, weight_zero, weight_first, weight_second):
    rows, grad, flat = edge_block(
        edge_count, source, target, rotation[0], radial[0], node_feats, cotangent, weight_zero, weight_first, weight_second)
    return tuple(finish(rows, grad, flat))


def solution(mesh):
    edge = P("dp", "graph")
    node = P("dp", "graph", None)
    return jax.shard_map(
        per_device,
        mesh=mesh,
        in_specs=(node, edge, edge, P("dp", None, "graph"), node, edge, node, P(), P(), P()),
        out_specs=(node, node, P(), P(), P()),
        check_vma=False,
    )
```

```python
import functools, math
import jax, jax.numpy as jnp, numpy as np
from jax import lax
from jax.experimental import pallas as pl
from jax.experimental.pallas import tpu as pltpu
from jax.sharding import PartitionSpec as P

C = 128
E = 128
N = 256
W = 25 * C
F32, BF16 = jnp.float32, jnp.bfloat16
OFF = [0, 1, 10, 35, 84]


def dot(a, b):
    return lax.dot_general(a, b, (((1,), (0,)), ((), ())), preferred_element_type=F32)


def dot_nt(a, b):
    return lax.dot_general(a, b, (((1,), (1,)), ((), ())), preferred_element_type=F32)


def dot_tn(a, b):
    return lax.dot_general(a, b, (((0,), (0,)), ((), ())), preferred_element_type=F32)


def orders(l):
    top = min(l, 2)
    return range(-top, top + 1)


def kept(l):
    return sum(len(orders(q)) * (2 * q + 1) for q in range(l))


def prepare(src, dst, count, rot, oh_s, oh_d, oh_st, oh_dt, rot_t):
    node = lax.broadcasted_iota(jnp.int32, (N, E), 0)
    slot = lax.broadcasted_iota(jnp.int32, (N, E), 1)
    s = (node == src).astype(F32)
    d = ((node == dst) & (slot < count)).astype(F32)
    oh_st[...] = s.astype(BF16)
    oh_dt[...] = d.astype(BF16)
    oh_s[...] = s.T.astype(BF16)
    oh_d[...] = d.T.astype(BF16)
    eye = (lax.broadcasted_iota(jnp.int32, (E, E), 0) == lax.broadcasted_iota(jnp.int32, (E, E), 1)).astype(BF16)
    k = lax.broadcasted_iota(jnp.int32, (1, 165), 1)
    scale = jnp.ones((1, 165), F32)
    for l in range(1, 5):
        scale = jnp.where(k >= OFF[l], 1.0 / math.sqrt(2 * l + 1), scale)
    rot_t[:, :165] = dot_nt(eye, rot) * scale


def group_slot(l, m):
    return abs(m), (E if m < 0 else 0), (l - abs(m)) * C


PARTS = (1, 1, 1, 2, 2)


def loop_parts(step, parts):
    for p in range(parts):
        if p:
            yield
        pl.loop(p * 8 // parts, (p + 1) * 8 // parts)(step)


def rotate_in(l, feats, cots, oh_s, oh_d, rad, rot_t, x_buf, u_buf, wide, act, ups, ups_s):
    size = 2 * l + 1
    cols = slice(l * l * C, (l + 1) * (l + 1) * C)
    x_buf[:, : size * C] = dot(oh_s[...], feats[:, :, :, cols].reshape(N, size * C))
    u_buf[:, : size * C] = dot(oh_d[...], cots[:, :, :, cols].reshape(N, size * C))

    def step(b):
        r = pl.multiple_of(b * 16, 16)
        rows = pl.ds(r, 16)
        rt = rot_t[rows, :]
        xs = [x_buf[rows, j * C : (j + 1) * C] for j in range(size)]
        us = [u_buf[rows, j * C : (j + 1) * C] for j in range(size)]
        rd = rad[rows, l * C : (l + 1) * C].astype(F32)
        at = kept(l)
        for m in orders(l):
            a = u = None
            for j in range(size):
                k = OFF[l] + (m + l) * size + j
                w = jnp.broadcast_to(rt[:, k : k + 1], (16, C))
                wide[at, rows, :] = w
                at += 1
                a = w * xs[j] if a is None else a + w * xs[j]
                u = w * us[j] if u is None else u + w * us[j]
            g, ro, co = group_slot(l, m)
            here = pl.ds(r + ro, 16)
            cols = slice(co, co + C)
            act[g][here, cols] = (a * rd).astype(BF16)
            ub = u.astype(BF16)
            ups[g][here, cols] = ub
            if g:
                there = pl.ds(r + E - ro, 16)
                ups_s[g][there, cols] = ub if m < 0 else -ub

    yield from loop_parts(step, PARTS[l])


def plane(act, ups, ws, msg, back):
    msg[0][...] = dot(act[0][...], ws[0][...])
    back[0][...] = dot_nt(ups[0][...], ws[0][...])
    for g in (1, 2):
        a = act[g][...]
        y0 = dot(a, ws[g][0])
        y1 = dot(a, ws[g][1])
        msg[g][:E, :] = y0[:E] - y1[E:]
        msg[g][E:, :] = y0[E:] + y1[:E]
        u = ups[g][...]
        z0 = dot_nt(u, ws[g][0])
        z1 = dot_nt(u, ws[g][1])
        back[g][:E, :] = z0[:E] + z1[E:]
        back[g][E:, :] = z0[E:] - z1[:E]


def rotate_out(l, msg, back, rad, wide, oh_st, oh_dt, m_buf, e_buf, out, grad):
    size = 2 * l + 1

    def step(b):
        r = pl.multiple_of(b * 16, 16)
        rows = pl.ds(r, 16)
        rd = rad[rows, l * C : (l + 1) * C].astype(F32)
        ms, bs = [], []
        for m in orders(l):
            g, ro, co = group_slot(l, m)
            here = pl.ds(r + ro, 16)
            ms.append(msg[g][here, co : co + C])
            bs.append(back[g][here, co : co + C] * rd)
        n = len(ms)
        for i in range(size):
            a = u = None
            for j in range(n):
                w = wide[kept(l) + j * size + i, rows, :]
                a = w * ms[j] if a is None else a + w * ms[j]
                u = w * bs[j] if u is None else u + w * bs[j]
            m_buf[rows, i * C : (i + 1) * C] = a.astype(BF16)
            e_buf[rows, i * C : (i + 1) * C] = u.astype(BF16)

    yield from loop_parts(step, PARTS[l])
    cols = slice(l * l * C, (l + 1) * (l + 1) * C)
    shape = (4, 4, 16, size * C)
    out[:, :, :, cols] = dot(oh_dt[...], m_buf[:, : size * C]).astype(BF16).reshape(shape)
    grad[:, :, :, cols] = dot(oh_st[...], e_buf[:, : size * C]).astype(BF16).reshape(shape)


def weight_grads(act, ups, ups_s, flat):
    scale = 1.0 / math.sqrt(32768)
    at = 0
    for g in range(3):
        left = act[g][...].T
        for right in (ups, ups_s)[: 1 if g == 0 else 2]:
            total = (dot(left, right[g][...]) * scale).astype(BF16)
            rows = total.shape[0]
            for c in range(rows // C):
                flat[at : at + rows // 16] = total[:, c * C : (c + 1) * C].reshape(rows // 16, 16, C)
                at += rows // 16
    flat[600:608] = jnp.zeros((8, 16, C), BF16)


MESH = pl.DeviceIdType.MESH
TILES = 304
HALVES = ((0, 10), (160, 9))


def start_at(z):
    return lax.div(z * 16, 7) if not isinstance(z, int) else z * 16 // 7


def wrap(p, d, n):
    return lax.rem(p + (d % n), n)


class Place:
    def __init__(self):
        g, p = lax.axis_index("graph"), lax.axis_index("dp")
        self.g, self.p = g, p
        self.y, self.x = lax.div(g, 4), lax.rem(g, 4)
        self.z, self.c = lax.div(p, 2), lax.rem(p, 2)

    def plane(self, dy, dx):
        return (self.p, wrap(self.y, dy, 4) * 4 + wrap(self.x, dx, 4))

    def peer(self, d):
        return (self.p, wrap(self.g, d, 16))

    def up(self, d):
        return (wrap(self.z, d, 8) * 2 + self.c, self.g)

    def sibling(self):
        return (self.z * 2 + 1 - self.c, self.g)


class Sender:
    def __init__(self, send, recv):
        self.send, self.recv, self.next, self.open, self.most = send, recv, 0, [], 0

    def go(self, src, dst, to):
        c = pltpu.make_async_remote_copy(src_ref=src, dst_ref=dst, send_sem=self.send.at[len(self.open)],
                                         recv_sem=self.recv.at[self.next], device_id=to, device_id_type=MESH)
        self.next += 1
        self.open.append(c)
        c.start()
        return c

    def drain(self):
        for c in self.open:
            c.wait_send()
        self.open = []


class Runner:
    def __init__(self):
        self.active = []

    def add(self, stream, delay=0):
        self.active.append([stream, delay])
        return stream

    def run(self):
        while self.active:
            for entry in list(self.active):
                if entry[1] > 0:
                    entry[1] -= 1
                    continue
                try:
                    next(entry[0])
                except StopIteration:
                    self.active.remove(entry)


def gather_stream(snd, at, dev):
    def spread(da):
        return [snd.go(at(da, 0, None), at(da, 0, None), dev(0, s)) for s in (1, -1)]

    def relay(da, got):
        for k, s in enumerate((1, -1)):
            yield
            got[k].wait_recv()
            last.append(snd.go(at(da, -s, k), at(da, -s, k), dev(0, s)))

    last = []
    first = {-s: snd.go(at(0, 0, None), at(0, 0, None), dev(s, 0)) for s in (1, -1)}
    second = {0: spread(0)}
    first[2] = snd.go(at(0, 0, None), at(0, 0, None), dev(2, 0))
    for da in (-1, 1):
        yield
        first[da].wait_recv()
        second[da] = spread(da)
    yield from relay(0, second[0])
    yield
    first[2].wait_recv()
    second[2] = spread(2)
    for da in (-1, 1, 2):
        yield from relay(da, second[da])
    for f in last:
        yield
        f.wait_recv()


def col_at(buf, here, lo, hi, y_first):
    mid = (lo + hi) // 2
    parts = {None: (lo, hi), 0: (lo, mid), 1: (mid, hi)}

    def at(da, db, part):
        dy, dx = (da, db) if y_first else (db, da)
        a, b = parts[part]
        return buf.at[wrap(here.y, dy, 4), wrap(here.x, dx, 4), :, a * C : b * C]
    return at


def plane_dev(here, y_first):
    return (lambda da, db: here.plane(da, db)) if y_first else (lambda da, db: here.plane(db, da))


def add(*xs):
    t = xs[0].astype(F32)
    for x in xs[1:]:
        t = t + x.astype(F32)
    return t.astype(BF16)


def scatter_stream(snd, part, mid, t, r, q, r2, out, here, lo, hi, y_first):
    cm = (lo + hi) // 2
    full, halves = slice(lo * C, hi * C), (slice(lo * C, cm * C), slice(cm * C, hi * C))
    a, b = (here.y, here.x) if y_first else (here.x, here.y)
    dev = plane_dev(here, y_first)

    def row(da, cols):
        i = wrap(a, da, 4)
        return part.at[i, :, :, cols] if y_first else part.at[:, i, :, cols]

    got = [snd.go(row(2, halves[k]), t.at[k, :, :, halves[k]], dev(s, 0)) for k, s in enumerate((1, -1))]
    sent = []
    for k, s in enumerate((1, -1)):
        yield
        got[k].wait_recv()
        mid[k, :, :, halves[k]] = add(row(s, halves[k])[...], t[k, :, :, halves[k]])
        mid[k, :, :, halves[1 - k]] = row(s, halves[1 - k])[...]
        sent.append(snd.go(mid.at[k, :, :, full], r.at[k, :, :, full], dev(s, 0)))
    yield
    sent[0].wait_recv()
    sent[1].wait_recv()
    q[:, :, full] = add(row(0, full)[...], r[0, :, :, full], r[1, :, :, full])
    sent = []
    for k, s in enumerate((2, 1, -1)):
        sent.append(snd.go(q.at[wrap(b, s, 4), :, full], r2.at[k, :, full], dev(0, s)))
    yield
    for c in sent:
        c.wait_recv()
    out[:, full] = add(q[b, :, full], *(r2[k, :, full] for k in range(3)))


def block(ref, base, size, a, b, count=1):
    return ref.at[pl.ds(base + (a * 4 + b) * size, size * count)]


def weight_start(snd, flat, sib, here):
    other = (1 - here.c) * TILES
    copies = {}
    for da in (2, 1, -1, 0):
        for part, (off, size) in enumerate(HALVES):
            a = wrap(here.y if part == 0 else here.x, da, 4)
            copies[part, da] = snd.go(block(flat, other + off, size, a, 0, 4), block(sib, off, size, a, 0, 4), here.sibling())
    return copies


def weight_plane(snd, copies, part, flat, sib, hsum, tbox, qsum, t2box, zin, here):
    off, size = HALVES[part]
    y_first = part == 0
    a, b = (here.y, here.x) if y_first else (here.x, here.y)
    dev = plane_dev(here, y_first)
    own = here.c * TILES
    sent = []
    for k, da in enumerate((2, 1, -1)):
        copies[part, da].wait_recv()
        i = wrap(a, da, 4)
        block(hsum, off, size, i, 0, 4)[...] = add(block(flat, own + off, size, i, 0, 4)[...], block(sib, off, size, i, 0, 4)[...])
        sent.append(snd.go(block(hsum, off, size, i, 0, 4), tbox.at[k, off // 4 : off // 4 + 4 * size], dev(da, 0)))
    copies[part, 0].wait_recv()
    yield
    for c in sent:
        c.wait_recv()
    rows = slice(off // 4, off // 4 + 4 * size)
    qsum[rows] = add(block(flat, own + off, size, a, 0, 4)[...], block(sib, off, size, a, 0, 4)[...], *(tbox[k, rows] for k in range(3)))
    sent = []
    for k, db in enumerate((2, 1, -1)):
        i = wrap(b, db, 4)
        sent.append(snd.go(qsum.at[pl.ds(off // 4 + i * size, size)], t2box.at[k, off // 16 : off // 16 + size], dev(0, db)))
    yield
    for c in sent:
        c.wait_recv()
    rows = slice(off // 16, off // 16 + size)
    zin[rows] = add(qsum[pl.ds(off // 4 + b * size, size)], *(t2box[k, rows] for k in range(3)))


def weight_z(snd, zin, zbox, zall, zout, res, here):
    copies = [snd.go(zin.at[pl.ds(start_at(wrap(here.z, d, 8)), 3)], zbox.at[d], here.up(d)) for d in range(1, 8)]
    yield
    total = zin[pl.ds(start_at(here.z), 3)].astype(F32)
    for d in range(1, 8):
        copies[d - 1].wait_recv()
        total = total + zbox[d].astype(F32)
    zall[here.z] = total.astype(BF16)
    copies = [snd.go(zall.at[here.z], zall.at[here.z], here.up(d)) for d in range(1, 8)]
    yield
    for c in copies:
        c.wait_recv()
    for z in range(8):
        zout[start_at(z) : start_at(z) + 3] = zall[z]
    for part, (off, size) in enumerate(HALVES):
        a, b = (here.y, here.x) if part == 0 else (here.x, here.y)
        block(res, here.c * TILES + off, size, a, b)[...] = zout[off // 16 : off // 16 + size]


def weight_spread(snd, part, res, here, cores):
    off, size = HALVES[part]
    y_first = part == 0
    a, b = (here.y, here.x) if y_first else (here.x, here.y)
    dev = plane_dev(here, y_first)

    def at(da, db):
        return block(res, here.c * TILES + off, size, wrap(a, da, 4), wrap(b, db, 4))

    def to_core(da):
        row = block(res, here.c * TILES + off, size, wrap(a, da, 4), 0, 4)
        cores.append(snd.go(row, row, here.sibling()))

    first = {-d % 4: snd.go(at(0, 0), at(0, 0), dev(d, 0)) for d in (1, -1, 2)}
    second = {}
    for db in (1, -1, 2):
        second[0, -db % 4] = snd.go(at(0, 0), at(0, 0), dev(0, db))
    for da in (1, 3, 2):
        yield
        first[da].wait_recv()
        for db in (1, -1, 2):
            second[da, -db % 4] = snd.go(at(da, 0), at(da, 0), dev(0, db))
    for da in (0, 1, 3, 2):
        yield
        for db in (1, 3, 2):
            second[da, db].wait_recv()
        to_core(da)


CHUNKS = (((0, 1, 2), 0), ((3,), 2), ((4,), 4))
RCHUNKS = ((4,), (3,), (0, 1, 2))
ORDER = "wnnwnwn"
FIRST = 1


def bounds(degrees):
    return degrees[0] ** 2, (degrees[-1] + 1) ** 2


def block_kernel(count, src_in, dst_in, rot_in, rad_in, f_in, c_in, w0_in, w1_in, w2_in, out, grad, res,
                 src, dst, rot, rad, f_buf, c_buf, oh_s, oh_d, oh_st, oh_dt, rot_t, x_buf, u_buf, wide, a0, a1, a2, u0, u1, u2, v1, v2,
                 m0, m1, m2, b0, b1, b2, mb, eb, w0, w1, w2, p_out, p_grad, mid, t, r, q, r2,
                 flat, sib, hsum, tbox, qsum, t2box, zin, zbox, zall, zout, send, recv, w_sem):
    here = Place()
    loads = [pltpu.make_async_copy(i, o, w_sem.at[k]) for k, (i, o) in enumerate((
        (f_in.at[0], f_buf.at[here.y, here.x]), (c_in.at[0], c_buf.at[here.y, here.x]), (src_in, src), (dst_in, dst),
        (rot_in, rot), (rad_in, rad), (w0_in, w0), (w1_in, w1), (w2_in, w2)))]
    for c in loads:
        c.start()
    partners = [here.sibling()] + [here.up(d) for d in range(1, 8)] + [
        here.plane(*d) for d in ((0, 1), (0, -1), (0, 2), (1, 0), (-1, 0), (2, 0))]
    barrier = pltpu.get_barrier_semaphore()
    for d in partners:
        pl.semaphore_signal(barrier, inc=1, device_id=d, device_id_type=MESH)
    for c in loads[:5]:
        c.wait()
    prepare(src[...], dst[...], count[0, 0], rot[...], oh_s, oh_d, oh_st, oh_dt, rot_t)
    pl.semaphore_wait(barrier, len(partners))
    loads[5].wait()

    act, ups, ups_s = (a0, a1, a2), (u0, u1, u2), (None, v1, v2)
    ws, msg, back = (w0, w1, w2), (m0, m1, m2), (b0, b1, b2)
    snd = Sender(send, recv)
    run = Runner()

    def take_in(degrees, parts):
        for p in parts:
            yield from p
        for l in degrees:
            yield
            yield from rotate_in(l, f_buf, c_buf, oh_s, oh_d, rad, rot_t, x_buf, u_buf, wide, act, ups, ups_s)

    def both(lo, hi):
        f = gather_stream(snd, col_at(f_buf, here, lo, hi, False), plane_dev(here, False))
        c = gather_stream(snd, col_at(c_buf, here, lo, hi, True), plane_dev(here, True))
        live = [f, c]
        while live:
            for s in list(live):
                try:
                    next(s)
                except StopIteration:
                    live.remove(s)
            if live:
                yield

    starts = []
    for degrees, delay in CHUNKS:
        stream = both(*bounds(degrees))
        next(stream)
        run.add(take_in(degrees, [stream]), delay)
    run.run()

    weight_grads(act, ups, ups_s, flat)
    snd.drain()
    copies = weight_start(snd, flat, sib, here)

    def turns(streams):
        live = list(streams)
        while live:
            for s in list(live):
                try:
                    next(s)
                except StopIteration:
                    live.remove(s)
            yield

    def weights():
        yield from turns([weight_plane(snd, copies, p, flat, sib, hsum, tbox, qsum, t2box, zin, here) for p in range(2)])
        yield from weight_z(snd, zin, zbox, zall, zout, res, here)
        cores = []
        yield from turns([weight_spread(snd, p, res, here, cores) for p in range(2)])
        for c in cores:
            c.wait_recv()

    sums = weights()
    rows = []
    for c in loads[6:]:
        c.wait()
    plane(act, ups, ws, msg, back)
    for k, degrees in enumerate(RCHUNKS):
        if k == FIRST:
            next(sums)
        for l in degrees:
            for _ in rotate_out(l, msg, back, rad, wide, oh_st, oh_dt, mb, eb, p_out, p_grad):
                pass
        lo, hi = bounds(degrees)
        for i, (part, dst_ref, yf) in enumerate(((p_out, out, True), (p_grad, grad, False))):
            rows.append(scatter_stream(snd, part, mid.at[i], t.at[i], r.at[i], q.at[i], r2.at[i], dst_ref, here, lo, hi, yf))
            next(rows[-1])
    for step in ORDER:
        if step == "w":
            next(sums, None)
        else:
            for s in rows:
                next(s, None)
    for _ in sums:
        pass
    snd.drain()


def edge_block(count, src, dst, rot, rad, feats, cots, w0, w1, w2):
    v = pl.BlockSpec(memory_space=pltpu.VMEM)
    h = pl.BlockSpec(memory_space=pltpu.HBM)
    V = pltpu.VMEM
    rows = jax.ShapeDtypeStruct((16, W), BF16)
    n_send, n_recv = 114, 228
    return pl.pallas_call(
        block_kernel,
        out_shape=(rows, rows, jax.ShapeDtypeStruct((2 * TILES, 16, C), BF16)),
        in_specs=[pl.BlockSpec(memory_space=pltpu.SMEM)] + [h] * 9,
        out_specs=(v,) * 3,
        scratch_shapes=[
            V((1, E), jnp.int32), V((1, E), jnp.int32), V((165, E), BF16), V((E, 640), BF16),
            V((4, 4, 16, W), BF16), V((4, 4, 16, W), BF16),
            V((E, N), BF16), V((E, N), BF16), V((N, E), BF16), V((N, E), BF16), V((E, 256), F32),
            V((E, 9 * C), F32), V((E, 9 * C), F32), V((115, E, C), F32),
            V((E, 640), BF16), V((2 * E, 512), BF16), V((2 * E, 384), BF16),
            V((E, 640), BF16), V((2 * E, 512), BF16), V((2 * E, 384), BF16),
            V((2 * E, 512), BF16), V((2 * E, 384), BF16),
            V((E, 640), F32), V((2 * E, 512), F32), V((2 * E, 384), F32),
            V((E, 640), F32), V((2 * E, 512), F32), V((2 * E, 384), F32),
            V((E, 9 * C), BF16), V((E, 9 * C), BF16),
            V((640, 640), BF16), V((2, 512, 512), BF16), V((2, 384, 384), BF16),
            V((4, 4, 16, W), BF16), V((4, 4, 16, W), BF16),
            V((2, 2, 4, 16, W), BF16), V((2, 2, 4, 16, W), BF16), V((2, 2, 4, 16, W), BF16), V((2, 4, 16, W), BF16),
            V((2, 3, 16, W), BF16),
            V((2 * TILES, 16, C), BF16), V((TILES, 16, C), BF16), V((TILES, 16, C), BF16), V((3, 76, 16, C), BF16),
            V((76, 16, C), BF16), V((3, 19, 16, C), BF16), V((19, 16, C), BF16), V((8, 3, 16, C), BF16), V((8, 3, 16, C), BF16),
            V((19, 16, C), BF16),
            pltpu.SemaphoreType.DMA((n_send,)), pltpu.SemaphoreType.DMA((n_recv,)), pltpu.SemaphoreType.DMA((9,)),
        ],
        compiler_params=pltpu.CompilerParams(collective_id=0, has_side_effects=True, vmem_limit_bytes=60 * 2**20),
        name="edge_block",
    )(count, src, dst, rot, rad, feats, cots, w0, w1, w2)


def finish_kernel(rows_in, grad_in, flat, rows, grad, g0, g1, g2):
    rows[0] = rows_in[...]
    grad[0] = grad_in[...]
    for c in range(5):
        g0[:, c * C : (c + 1) * C] = flat[c * 40 : c * 40 + 40].reshape(640, C).astype(F32)
    for i in range(2):
        for c in range(4):
            b = 200 + i * 128 + c * 32
            g1[i, :, c * C : (c + 1) * C] = flat[b : b + 32].reshape(512, C).astype(F32)
        for c in range(3):
            b = 456 + i * 72 + c * 24
            g2[i, :, c * C : (c + 1) * C] = flat[b : b + 24].reshape(384, C).astype(F32)


def finish(rows, grad, flat):
    v = pl.BlockSpec(memory_space=pltpu.VMEM)
    o = jax.ShapeDtypeStruct((1, 16, W), BF16)
    return pl.pallas_call(
        finish_kernel,
        out_shape=(o, o, jax.ShapeDtypeStruct((640, 640), F32), jax.ShapeDtypeStruct((2, 512, 512), F32),
                   jax.ShapeDtypeStruct((2, 384, 384), F32)),
        in_specs=[v] * 3, out_specs=(v,) * 5,
        compiler_params=pltpu.CompilerParams(vmem_limit_bytes=60 * 2**20),
        name="finish",
    )(rows, grad, flat)


def per_device(node_feats, source, target, rotation, radial, edge_count, cotangent, weight_zero, weight_first, weight_second):
    rows, grad, flat = edge_block(
        edge_count, source, target, rotation[0], radial[0], node_feats, cotangent, weight_zero, weight_first, weight_second)
    return tuple(finish(rows, grad, flat))


def solution(mesh):
    edge = P("dp", "graph")
    node = P("dp", "graph", None)
    return jax.shard_map(
        per_device,
        mesh=mesh,
        in_specs=(node, edge, edge, P("dp", None, "graph"), node, edge, node, P(), P(), P()),
        out_specs=(node, node, P(), P(), P()),
        check_vma=False,
    )
```
